256 devices in a mesh: group: 32 (over y, z_lo, core), dp: 8 (over x, z_hi).
Axes of the slice: x: 4, y: 4, z: 8 (z_hi: 2, z_lo: 4; z = z_hi * 4 + z_lo), core: 2. Of those that a mesh axis runs over, the one named last changes fastest.
Arguments:
- tokens: bfloat16 [32768, 3584], P(('group', 'dp')), may hold values from -6 to 6
- routes: int32 [32768, 1], P(('group', 'dp')), may hold values from 0 to 7; in each aligned block of 128 rows (0 to 127, 128 to 255, ...) at most 24 rows name the same one
- gate_scale: float32 [32768, 1], P(('group', 'dp')), may hold values from 0.1 to 1
- cotangent: bfloat16 [32768, 3584], P(('group', 'dp')), may hold values from -0.59765625 to 0.59765625
- master: float32 [32, 256, 10752], P('group', 'dp'), may hold values from -0.09375 to 0.09375
- moment_one: float32 [32, 256, 10752], P('group', 'dp'), may hold values from -3 to 3
- moment_two: float32 [32, 256, 10752], P('group', 'dp'), may hold values from 0.01 to 1
- dec_tokens: bfloat16 [4, 512, 3584], P(None, 'group'), may hold values from -6 to 6
- dec_routes: int32 [4, 512, 1], P(None, 'group'), may hold values from 0 to 7; in each aligned block of 16 rows (0 to 15, 16 to 31, ..., all dimensions but the last counted through in order) at most 4 rows name the same one
- dec_scale: float32 [4, 512, 1], P(None, 'group'), may hold values from 0.5 to 2
Outputs:
- new_master: float32 [32, 256, 10752], P('group', 'dp')
- new_moment_one: float32 [32, 256, 10752], P('group', 'dp')
- new_moment_two: float32 [32, 256, 10752], P('group', 'dp')
- dec_out: bfloat16 [4, 512, 3584], P(None, 'group', 'dp')
The draws below stay inside these ranges and needn't reach their ends.
Inputs may be any that keep to these rules, and one draw needn't show every extreme that they name: `routes`: in each aligned block of 128 rows (the rows of one device) no expert is named by more than 24 rows; in some blocks one expert is named by exactly 24. `dec_routes`: within one step, in each aligned block of 16 rows (the rows of one index of group) no expert is named by more than 4 rows; in some blocks one expert is named by exactly 4.
All inputs are finite; a program needn't handle non-finite values.
Results may differ from the reference program's by a relative error of at most 0.0076.
Values may be sent and summed in bfloat16 or wider, within the bound.
No kernel may reach another device: no remote copies, remote signals or barrier semaphores. Data moves between devices by JAX's collectives and lax.ppermute only.
A program may use at most 128 MiB of HBM per device.

```python
import math
import jax
import jax.numpy as jnp
import numpy as np
from jax import lax

D = 3584
EXPERTS = 8
STEPS = 4
TOK_DEV = 128
DEC_DEV = 16
FF_SLICE = 256
CAP = 24
DCAP = 4
TOKENS = 32768
DEC_ROWS = 512
N_GROUP = 32
N_DP = 8


def levels(key, shape, shards, smallest, top_value):
    level = 1.0
    for axis_at, blocks in shards:
        heights = jax.random.uniform(jax.random.fold_in(jax.random.fold_in(key, 6), axis_at), (blocks,), jnp.float32, smallest / len(shards), top_value / len(shards))
        level = level * jnp.repeat(jnp.exp(heights), shape[axis_at] // blocks).reshape((-1,) + (1,) * (len(shape) - 1 - axis_at))
    return level


def deal_out(stream_key, own, number, rows, amount, top, limit, slope):
    sequence = jax.random.permutation(stream_key, amount)
    packed, usual = load_shares(amount, rows * top, limit, slope, True), load_shares(amount, rows * top, limit, slope, False)
    places = jnp.arange(amount)

    def named(lengths, rotation):
        used = int((lengths > 0).sum())
        fixed = max(1, used // 4)
        passed = fixed + (places - fixed + rotation * (used - fixed)) % max(1, amount - fixed)
        return jnp.zeros((amount,), jnp.int32).at[sequence[jnp.where(places < fixed, places, passed)]].set(jnp.asarray(lengths, jnp.int32))

    lengths = jnp.where(number % 4 == 0, named(packed, number // 4), named(usual, number - number // 4 - 1))
    mixed = jax.random.permutation(jax.random.fold_in(own, 3), amount)
    giver, receiver = mixed[0:amount // 2 * 2:2], mixed[1:amount // 2 * 2:2]
    room = jnp.minimum(lengths[giver] - 1, limit - lengths[receiver]) // 2
    room = jnp.where((giver == sequence[0]) | (receiver == sequence[0]) | (lengths[receiver] == 0), 0, jnp.maximum(room, 0))
    passed = jax.random.randint(jax.random.fold_in(own, 4), (amount // 2,), 0, 1 << 20) % (room + 1)
    lengths = lengths.at[giver].add(-passed).at[receiver].add(passed)
    items = jnp.searchsorted(jnp.cumsum(lengths), jnp.arange(rows * top), side="right").astype(jnp.int32)
    table = items.reshape(top, rows).T
    table = table[jax.random.permutation(jax.random.fold_in(own, 1), rows)]
    rotation = jax.random.randint(jax.random.fold_in(own, 2), (rows, 1), 0, top)
    return jnp.take_along_axis(table, (jnp.arange(top)[None, :] + rotation) % top, axis=1)


def load_shares(number_of, total, bound, lean, full):
    portions = [(1 << 20) // math.isqrt(standing ** lean) + 1 for standing in range(1, number_of + 1)]
    largest = bound if full else min(bound, max(-(-total // number_of), total * portions[0] // sum(portions)))
    least = 1 if total - largest >= number_of - 1 else 0
    given, spare = [largest] + [least] * (number_of - 1), total - largest - least * (number_of - 1)
    while spare > 0:
        free = [i for i in range(1, number_of) if given[i] < largest] or [i for i in range(1, number_of) if given[i] < bound]
        mass, budget = sum([portions[i] for i in free]), spare
        for i in free:
            addition = min(bound - given[i], max(1, budget * portions[i] // mass), spare)
            given[i] = given[i] + addition
            spare = spare - addition
    return np.array(given)


def gaussian(rng, shape, width, limit, pieces=(), held_as=jnp.bfloat16):
    level = levels(rng, shape, pieces, -0.22, 0.18) if pieces else 1.0
    values = jax.random.normal(rng, shape, jnp.float32) * width * level
    return jnp.minimum(jnp.maximum(values, -limit), limit).astype(held_as)


def setup_inputs(seed: int = 0) -> dict:
    key_of = jax.random.split(jax.random.key(seed), 11)
    tokens = gaussian(key_of[0], (TOKENS, D), 1.0, 6.0, ((0, 256),))
    routes_keys = jax.random.split(jax.random.fold_in(key_of[1], 1), TOKENS // TOK_DEV)
    routes_turns = jax.random.permutation(jax.random.fold_in(key_of[1], 3), TOKENS // TOK_DEV)
    routes = jax.vmap(lambda own, number: deal_out(jax.random.fold_in(key_of[1], 2), own, number, TOK_DEV, EXPERTS, 1, CAP, 2))(routes_keys, routes_turns).reshape((TOKENS, 1))
    gate_scale = jnp.clip(jnp.exp(math.log(1.0) - 2.3025851 * jax.random.uniform(key_of[2], (TOKENS, 1), jnp.float32) ** levels(key_of[2], (TOKENS, 1), ((0, 256),), -0.2, 0.2)), 0.1, 1.0)
    cotangent = gaussian(key_of[3], (TOKENS, D), 0.1, 0.59765625, ((0, 256),))
    master = gaussian(key_of[4], (N_GROUP, FF_SLICE, 3 * D), D ** -0.5, 0.09375, ((0, 32), (1, 8)), jnp.float32)
    moment_one = gaussian(key_of[5], (N_GROUP, FF_SLICE, 3 * D), 0.5, 3.0, ((0, 32), (1, 8)), jnp.float32)
    moment_two = jnp.clip(jnp.exp(math.log(1.0) - 4.6051702 * jax.random.uniform(key_of[6], (N_GROUP, FF_SLICE, 3 * D), jnp.float32) ** levels(key_of[6], (N_GROUP, FF_SLICE, 3 * D), ((0, 32), (1, 8)), -0.2, 0.2)), 0.01, 1.0)
    dec_tokens = gaussian(key_of[7], (STEPS, DEC_ROWS, D), 1.0, 6.0, ((1, 32),))
    dec_routes_keys = jax.random.split(jax.random.fold_in(key_of[8], 1), STEPS * DEC_ROWS // DEC_DEV)
    dec_routes_turns = jax.random.permutation(jax.random.fold_in(key_of[8], 3), STEPS * DEC_ROWS // DEC_DEV)
    dec_routes = jax.vmap(lambda own, number: deal_out(jax.random.fold_in(key_of[8], 2), own, number, DEC_DEV, EXPERTS, 1, DCAP, 2))(dec_routes_keys, dec_routes_turns).reshape((STEPS, DEC_ROWS, 1))
    dec_scale = jnp.clip(jnp.exp(math.log(2.0) - 1.3862944 * jax.random.uniform(key_of[9], (STEPS, DEC_ROWS, 1), jnp.float32) ** levels(key_of[9], (STEPS, DEC_ROWS, 1), ((1, 32),), -0.2, 0.2)), 0.5, 2.0)
    return {"tokens": tokens, "routes": routes, "gate_scale": gate_scale, "cotangent": cotangent, "master": master, "moment_one": moment_one, "moment_two": moment_two, "dec_tokens": dec_tokens, "dec_routes": dec_routes, "dec_scale": dec_scale}


adam_lr = 0.001
beta_one = 0.9
beta_two = 0.95
adam_eps = 1e-08
decay_rate = 0.1
step_count = 100.0

def silu_parts(values):
    sig = jax.nn.sigmoid(values)
    return (values * sig, sig * (1.0 + values * (1.0 - sig)))

def by_expert(array):
    split = N_GROUP // EXPERTS
    shaped = array.reshape(split, EXPERTS, FF_SLICE, 3 * D)
    return jnp.transpose(shaped, (1, 0, 2, 3)).reshape(EXPERTS, split * FF_SLICE, 3 * D)

def reference(tokens, routes, gate_scale, cotangent, master, moment_one, moment_two, dec_tokens, dec_routes, dec_scale):
    split = N_GROUP // EXPERTS
    scaled = (gate_scale * cotangent.astype(jnp.float32)).astype(jnp.bfloat16)
    route_ids = routes[:, 0]
    total_cap = CAP * N_GROUP * N_DP
    expert_weights = by_expert(master.astype(jnp.bfloat16))

    def one_expert(expert):
        chosen = route_ids == expert
        index = jnp.nonzero(chosen, size=total_cap, fill_value=0)[0]
        valid = jnp.arange(total_cap) < jnp.sum(chosen.astype(jnp.int32))
        x_rows = jnp.where(valid[:, None], tokens[index], jnp.zeros((), jnp.bfloat16))
        d_rows = jnp.where(valid[:, None], scaled[index], jnp.zeros((), jnp.bfloat16))
        w_exp = lax.dynamic_index_in_dim(expert_weights, expert, 0, keepdims=False)
        gate_pre = jnp.dot(x_rows, w_exp[:, :D].T, preferred_element_type=jnp.float32)
        up_pre = jnp.dot(x_rows, w_exp[:, D:2 * D].T, preferred_element_type=jnp.float32)
        back_pre = jnp.dot(d_rows, w_exp[:, 2 * D:].T, preferred_element_type=jnp.float32)
        silu_val, silu_grad = silu_parts(gate_pre)
        activated = (silu_val * up_pre).astype(jnp.bfloat16)
        grad_up = (back_pre * silu_val).astype(jnp.bfloat16)
        grad_gate = (back_pre * up_pre * silu_grad).astype(jnp.bfloat16)
        return jnp.concatenate([jnp.dot(grad_gate.T, x_rows, preferred_element_type=jnp.float32), jnp.dot(grad_up.T, x_rows, preferred_element_type=jnp.float32), jnp.dot(activated.T, d_rows, preferred_element_type=jnp.float32)], axis=1)
    per_expert = lax.map(one_expert, jnp.arange(EXPERTS, dtype=jnp.int32))
    grads = jnp.transpose(per_expert.reshape(EXPERTS, split, FF_SLICE, 3 * D), (1, 0, 2, 3)).reshape(N_GROUP, FF_SLICE, 3 * D)
    new_moment_one = beta_one * moment_one + (1.0 - beta_one) * grads
    new_moment_two = beta_two * moment_two + (1.0 - beta_two) * grads * grads
    correct_one = 1.0 - beta_one ** step_count
    correct_two = 1.0 - beta_two ** step_count
    update = new_moment_one / correct_one / (jnp.sqrt(new_moment_two / correct_two) + adam_eps)
    new_master = master - adam_lr * (update + decay_rate * master)
    rollout = by_expert(new_master.astype(jnp.bfloat16))
    flat_x = dec_tokens.reshape(STEPS * DEC_ROWS, D)
    flat_ids = dec_routes.reshape(STEPS * DEC_ROWS)
    dec_total = STEPS * DCAP * N_GROUP

    def add_expert(carry, expert):
        chosen = flat_ids == expert
        index = jnp.nonzero(chosen, size=dec_total, fill_value=0)[0]
        valid = jnp.arange(dec_total) < jnp.sum(chosen.astype(jnp.int32))
        x_rows = flat_x[index]
        w_exp = lax.dynamic_index_in_dim(rollout, expert, 0, keepdims=False)
        dec_gate = jnp.dot(x_rows, w_exp[:, :D].T, preferred_element_type=jnp.float32)
        dec_up = jnp.dot(x_rows, w_exp[:, D:2 * D].T, preferred_element_type=jnp.float32)
        silu_val, unused_grad = silu_parts(dec_gate)
        dec_act = (silu_val * dec_up).astype(jnp.bfloat16)
        expert_out = jnp.dot(dec_act, w_exp[:, 2 * D:], preferred_element_type=jnp.float32).astype(jnp.bfloat16)
        expert_out = lax.optimization_barrier(expert_out).astype(jnp.float32)
        carry = carry.at[index].add(jnp.where(valid[:, None], expert_out, jnp.zeros((), jnp.float32)))
        return (carry, None)
    start_rows = jnp.zeros((STEPS * DEC_ROWS, D), jnp.float32)
    combined, unused_out = lax.scan(add_expert, start_rows, jnp.arange(EXPERTS, dtype=jnp.int32))
    dec_out = (dec_scale.reshape(STEPS * DEC_ROWS, 1) * combined).astype(jnp.bfloat16).reshape(STEPS, DEC_ROWS, D)
    return (new_master, new_moment_one, new_moment_two, dec_out)
```

```python
import jax
import jax.numpy as jnp
from jax import lax
from jax.sharding import PartitionSpec as P

EXPERTS = 8
CAP = 24
DCAP = 4
NY, NZ, NC, NX = 4, 8, 2, 4
HALF_Z = 4
ALL = ("group", "dp")

adam_lr = 0.001
beta_one = 0.9
beta_two = 0.95
adam_eps = 1e-08
decay_rate = 0.1
step_count = 100.0


def device_at(y, z, c, x):
    y, z, x = y % NY, z % NZ, x % NX
    group = (y * HALF_Z + z % HALF_Z) * NC + c
    return group * (NX * 2) + x * 2 + z // HALF_Z


def moved(value, dy=0, dz=0, swap_core=False, dx=0):
    pairs = []
    for y in range(NY):
        for z in range(NZ):
            for c in range(NC):
                for x in range(NX):
                    target = device_at(y + dy, z + dz, 1 - c if swap_core else c, x + dx)
                    pairs.append((device_at(y, z, c, x), target))
    return lax.ppermute(value, ALL, pairs)


def silu_parts(values):
    sig = jax.nn.sigmoid(values)
    return (values * sig, sig * (1.0 + values * (1.0 - sig)))


def rank_within(route_ids, experts, axis_dim):
    onehot = (route_ids[..., None] == jnp.arange(experts, dtype=jnp.int32)).astype(jnp.int32)
    running = jnp.cumsum(onehot, axis=axis_dim) - 1
    return jnp.sum(running * onehot, axis=-1)


def contract_rows(left, right):
    return lax.dot_general(
        left, right, (((1,), (1,)), ((), ())), preferred_element_type=jnp.float32
    )


def sum_rows(left, right):
    return lax.dot_general(
        left, right, (((0,), (0,)), ((), ())), preferred_element_type=jnp.float32
    )


def ring_gather(value, axis):
    half = value.shape[0] // 2
    below = moved(value, **{axis: 1})
    above = moved(value, **{axis: -1})
    far_first = moved(below[:half], **{axis: 1})
    far_second = moved(above[half:], **{axis: -1})
    return [value, below, above, far_first, far_second]


def ring_scatter(part):
    rows = part.shape[0] // 4
    half = rows // 2
    sent = part.astype(jnp.bfloat16)
    far = sent[3 * rows :]
    via_above = moved(far[:half], dx=1)
    via_below = moved(far[half:], dx=-1)
    up_first = (part[2 * rows : 2 * rows + half] + via_above.astype(jnp.float32)).astype(jnp.bfloat16)
    down_second = (part[rows + half : 2 * rows] + via_below.astype(jnp.float32)).astype(jnp.bfloat16)
    from_below = moved(jnp.concatenate([up_first, sent[2 * rows + half : 3 * rows]], 0), dx=1)
    from_above = moved(jnp.concatenate([sent[rows : rows + half], down_second], 0), dx=-1)
    total = part[:rows] + from_below.astype(jnp.float32) + from_above.astype(jnp.float32)
    other = moved(total[half:].astype(jnp.bfloat16), dz=HALF_Z)
    return total[:half] + other.astype(jnp.float32)


def shards(
    tokens,
    routes,
    gate_scale,
    cotangent,
    master,
    moment_one,
    moment_two,
    dec_tokens,
    dec_routes,
    dec_scale,
):
    replicas = lax.axis_size("dp")
    groups = lax.axis_size("group")
    width = tokens.shape[1]
    own_group = lax.axis_index("group")
    own_expert = own_group % EXPERTS
    own_z, own_c = own_expert // NC, own_expert % NC

    route_ids = routes[:, 0]
    slot = rank_within(route_ids, EXPERTS, 0)
    scaled = (gate_scale * cotangent.astype(jnp.float32)).astype(jnp.bfloat16)
    other_core = (route_ids % NC) ^ own_c
    ahead = (route_ids // NC - own_z) % HALF_Z
    position = (other_core * HALF_Z + ahead) * CAP + slot
    select = (
        jnp.arange(EXPERTS * CAP, dtype=jnp.int32)[:, None] == position[None, :]
    ).astype(jnp.bfloat16)
    packed = jnp.concatenate(
        [
            jnp.dot(select, tokens, preferred_element_type=jnp.float32),
            jnp.dot(select, scaled, preferred_element_type=jnp.float32),
        ],
        1,
    ).astype(jnp.bfloat16)
    mine = packed[: HALF_Z * CAP]
    theirs = moved(packed[HALF_Z * CAP :], swap_core=True)

    def both(at):
        return jnp.concatenate(
            [mine[at * CAP : (at + 1) * CAP], theirs[at * CAP : (at + 1) * CAP]], 0
        )

    first = both(0)
    second = jnp.concatenate([moved(both(1), dz=1), moved(both(3), dz=-1)], 0)
    third = jnp.concatenate(
        [
            moved(mine[2 * CAP : 3 * CAP], dz=2),
            moved(theirs[2 * CAP : 3 * CAP], dz=-2),
        ],
        0,
    )
    rows = []
    for piece in (first, second, third):
        rows += ring_gather(piece, "dy")
    rows = jnp.concatenate(rows, 0)
    x_rows, d_rows = rows[:, :width], rows[:, width:]

    master_rows = master[0]
    weights = []
    for part in range(3):
        own = master_rows[:, part * width : (part + 1) * width].astype(jnp.bfloat16)
        pair = jnp.concatenate([own, moved(own, dz=HALF_Z)], 0)
        weights.append(jnp.concatenate(ring_gather(pair, "dx"), 0))
    gate_pre = contract_rows(x_rows, weights[0])
    up_pre = contract_rows(x_rows, weights[1])
    back_pre = contract_rows(d_rows, weights[2])
    silu_val, silu_grad = silu_parts(gate_pre)
    activated = (silu_val * up_pre).astype(jnp.bfloat16)
    grad_up = (back_pre * silu_val).astype(jnp.bfloat16)
    grad_gate = (back_pre * up_pre * silu_grad).astype(jnp.bfloat16)

    per_peer = DCAP // NY
    steps, dec_dev = dec_tokens.shape[0], dec_tokens.shape[1]
    dec_ids = dec_routes[..., 0]
    dec_slot = rank_within(dec_ids, EXPERTS, 1)
    block = (dec_slot // per_peer + own_group) % NY
    target = block * EXPERTS + dec_ids
    dec_position = (target * steps + jnp.arange(steps, dtype=jnp.int32)[:, None]) * per_peer
    dec_position = (dec_position + dec_slot % per_peer).reshape(steps * dec_dev)
    dec_slots = groups * steps * per_peer
    dec_select = (
        jnp.arange(dec_slots, dtype=jnp.int32)[:, None] == dec_position[None, :]
    ).astype(jnp.bfloat16)
    dec_packed = jnp.dot(
        dec_select, dec_tokens.reshape(steps * dec_dev, width), preferred_element_type=jnp.float32
    ).astype(jnp.bfloat16)
    dec_rows = lax.all_to_all(
        dec_packed.reshape(groups, steps * per_peer, width), "group", 0, 0, tiled=True
    ).reshape(dec_slots, width)

    correct_one = 1.0 - beta_one**step_count
    correct_two = 1.0 - beta_two**step_count
    new_master, new_one, new_two, rollout = [], [], [], []
    for part, (source, operand) in enumerate(
        ((grad_gate, x_rows), (grad_up, x_rows), (activated, d_rows))
    ):
        columns = slice(part * width, (part + 1) * width)
        grads = ring_scatter(sum_rows(source, operand))
        one = beta_one * moment_one[0, :, columns] + (1.0 - beta_one) * grads
        two = beta_two * moment_two[0, :, columns] + (1.0 - beta_two) * grads * grads
        update = one / correct_one / (jnp.sqrt(two / correct_two) + adam_eps)
        held = master_rows[:, columns]
        held = held - adam_lr * (update + decay_rate * held)
        new_one.append(one)
        new_two.append(two)
        new_master.append(held)
        rollout.append(jnp.concatenate(ring_gather(held.astype(jnp.bfloat16), "dy"), 0))

    dec_gate = contract_rows(dec_rows, rollout[0])
    dec_up = contract_rows(dec_rows, rollout[1])
    dec_act = (silu_parts(dec_gate)[0] * dec_up).astype(jnp.bfloat16)
    partial = jnp.dot(dec_act, rollout[2], preferred_element_type=jnp.float32).astype(jnp.bfloat16)
    out_width = width // replicas
    span = steps * per_peer
    partial = partial.reshape(groups, span, replicas, out_width).transpose(0, 2, 1, 3)
    partial = partial.reshape(groups * replicas, span * out_width)
    returned = lax.all_to_all(partial, ALL, 0, 0, tiled=True)
    returned = returned.reshape(groups, replicas, span * out_width).astype(jnp.float32)
    expert_out = jnp.sum(returned, 1).astype(jnp.bfloat16).reshape(dec_slots, out_width)
    picked = lax.dot_general(
        dec_select, expert_out, (((0,), (0,)), ((), ())), preferred_element_type=jnp.float32
    ).reshape(steps, dec_dev, out_width)
    dec_out = (dec_scale * picked).astype(jnp.bfloat16)
    return (
        jnp.concatenate(new_master, 1)[None],
        jnp.concatenate(new_one, 1)[None],
        jnp.concatenate(new_two, 1)[None],
        dec_out,
    )


def solution(mesh):
    in_specs = (
        P(("group", "dp"), None),
        P(("group", "dp"), None),
        P(("group", "dp"), None),
        P(("group", "dp"), None),
        P("group", "dp", None),
        P("group", "dp", None),
        P("group", "dp", None),
        P(None, "group", None),
        P(None, "group", None),
        P(None, "group", None),
    )
    out_specs = (
        P("group", "dp", None),
        P("group", "dp", None),
        P("group", "dp", None),
        P(None, "group", "dp"),
    )
    return jax.shard_map(shards, mesh=mesh, in_specs=in_specs, out_specs=out_specs, check_vma=False)
```

```python
import functools

import jax
import jax.numpy as jnp
from jax import lax
from jax.experimental import pallas as pl
from jax.experimental.pallas import tpu as pltpu
from jax.sharding import PartitionSpec as P

EXPERTS = 8
CAP = 24
DCAP = 4
NY, NZ, NC, NX = 4, 8, 2, 4
HALF_Z = 4
ALL = ("group", "dp")

adam_lr = 0.001
beta_one = 0.9
beta_two = 0.95
adam_eps = 1e-08
decay_rate = 0.1
step_count = 100.0


def device_at(y, z, c, x):
    y, z, x = y % NY, z % NZ, x % NX
    group = (y * HALF_Z + z % HALF_Z) * NC + c
    return group * (NX * 2) + x * 2 + z // HALF_Z


def moved(value, dy=0, dz=0, swap_core=False, dx=0):
    pairs = []
    for y in range(NY):
        for z in range(NZ):
            for c in range(NC):
                for x in range(NX):
                    target = device_at(y + dy, z + dz, 1 - c if swap_core else c, x + dx)
                    pairs.append((device_at(y, z, c, x), target))
    return lax.ppermute(value, ALL, pairs)


def silu_parts(values):
    sig = jax.nn.sigmoid(values)
    return (values * sig, sig * (1.0 + values * (1.0 - sig)))


def rank_within(route_ids, experts, axis_dim):
    onehot = (route_ids[..., None] == jnp.arange(experts, dtype=jnp.int32)).astype(jnp.int32)
    running = jnp.cumsum(onehot, axis=axis_dim) - 1
    return jnp.sum(running * onehot, axis=-1)


def contract_rows(left, right):
    return lax.dot_general(
        left, right, (((1,), (1,)), ((), ())), preferred_element_type=jnp.float32
    )


def assemble(recipes, after=()):
    arrays, places = [], {}
    for recipe in recipes:
        for segment in recipe:
            for array, _, _ in segment:
                if id(array) not in places:
                    places[id(array)] = len(arrays)
                    arrays.append(array)
    heights = [sum(segment[0][2] for segment in recipe) for recipe in recipes]
    count = len(arrays) + len(after)
    width = arrays[0].shape[1]
    blocks = 2

    def columns(rows):
        return pl.BlockSpec((rows, width // blocks), lambda i: (0, i))

    def body(*refs):
        for out, recipe in enumerate(recipes):
            at = 0
            for segment in recipe:
                values = [refs[places[id(v)]][start : start + rows] for v, start, rows in segment]
                if len(values) > 1:
                    total = values[0].astype(jnp.float32)
                    for value in values[1:]:
                        total += value.astype(jnp.float32)
                    values = [total.astype(jnp.bfloat16)]
                rows = segment[0][2]
                refs[count + out][at : at + rows] = values[0]
                at += rows

    return pl.pallas_call(
        body,
        grid=(blocks,),
        in_specs=[columns(v.shape[0]) for v in arrays]
        + [pl.BlockSpec(memory_space=pl.ANY)] * len(after),
        out_specs=[columns(h) for h in heights],
        out_shape=[jax.ShapeDtypeStruct((h, width), jnp.bfloat16) for h in heights],
        cost_estimate=pl.CostEstimate(
            flops=0, bytes_accessed=4 * sum(heights) * width, transcendentals=0
        ),
        name="assemble",
    )(*arrays, *after)


def pack_block(cap, select_ref, x_own, x_other, d_own, d_other, near, up, down, far_up, far_down):
    pairs = []
    for own, other in ((x_own, x_other), (d_own, d_other)):
        rows = jnp.concatenate([own[...], other[...]], 0)
        pairs.append(jnp.dot(select_ref[...], rows, preferred_element_type=jnp.float32))
    span = 2 * cap
    for out, at in ((near, 0), (up, 1), (down, 3)):
        out[:span] = pairs[0][at * span : (at + 1) * span].astype(jnp.bfloat16)
        out[span:] = pairs[1][at * span : (at + 1) * span].astype(jnp.bfloat16)
    for out, at in ((far_up, 2 * span), (far_down, 2 * span + cap)):
        out[...] = jnp.concatenate([v[at : at + cap] for v in pairs], 0).astype(jnp.bfloat16)


def pack(cap, select, *rows):
    width = rows[0].shape[1]
    blocks = 4
    block = width // blocks

    def columns(count):
        return pl.BlockSpec((count, block), lambda i: (0, i))

    heights = [4 * cap, 4 * cap, 4 * cap, 2 * cap, 2 * cap]
    return pl.pallas_call(
        functools.partial(pack_block, cap),
        grid=(blocks,),
        in_specs=[pl.BlockSpec(select.shape, lambda i: (0, 0))] + [columns(v.shape[0]) for v in rows],
        out_specs=[columns(h) for h in heights],
        out_shape=[jax.ShapeDtypeStruct((h, width), jnp.bfloat16) for h in heights],
        cost_estimate=pl.CostEstimate(
            flops=4 * select.size * width, bytes_accessed=2 * (4 * 128 + sum(heights)) * width, transcendentals=0
        ),
        name="pack",
    )(select, *rows)


def forward_block(places, count, own_x_ref, *refs):
    pieces, gate_ref, rest_ref = refs[:count], refs[count], refs[count + 1]
    outs, sums = refs[count + 2 : -3], refs[-3:]
    step = pl.program_id(0)
    for out, recipe in zip(outs[:2], places):
        at = 0
        for segment in recipe:
            values = [pieces[i][start : start + rows] for i, start, rows in segment]
            if len(values) > 1:
                values = [v.astype(jnp.float32) for v in values]
                values = [jnp.concatenate(values, 0).astype(jnp.bfloat16)]
            out[at : at + values[0].shape[0]] = values[0]
            at += values[0].shape[0]
    unit = rest_ref.shape[0] // (2 * NX)
    parts = [gate_ref[...]]
    for i in range(2):
        cuts = [rest_ref[(2 * x + i) * unit : (2 * x + i + 1) * unit] for x in range(NX)]
        parts.append(jnp.concatenate(cuts, 0))
    for total, part, rows in zip(sums, parts, (outs[0], outs[0], outs[1])):
        product = contract_rows(part, rows[...])

        @pl.when(step == 0)
        def _():
            total[...] = product

        @pl.when(step > 0)
        def _():
            total[...] += product

    @pl.when(step == pl.num_programs(0) - 1)
    def _():
        for x in range(NX):
            cut = slice(x * unit, (x + 1) * unit)
            gate_pre, up_pre, back_pre = (total[cut] for total in sums)
            silu_val, silu_grad = silu_parts(gate_pre)
            ahead = (x - own_x_ref[0] + NX) % NX
            to = pl.ds(pl.multiple_of(ahead * unit, unit), unit)
            outs[2][to] = (back_pre * up_pre * silu_grad).astype(jnp.bfloat16)
            outs[3][to] = (back_pre * silu_val).astype(jnp.bfloat16)
            outs[4][to] = (silu_val * up_pre).astype(jnp.bfloat16)


def forward(x_recipe, d_recipe, gate, rest, own_x):
    arrays, index = [], {}
    for recipe in (x_recipe, d_recipe):
        for segment in recipe:
            for array, _, _ in segment:
                if id(array) not in index:
                    index[id(array)] = len(arrays)
                    arrays.append(array)
    places = [
        [[(index[id(v)], start, rows) for v, start, rows in segment] for segment in recipe]
        for recipe in (x_recipe, d_recipe)
    ]
    height = sum(rows for segment in x_recipe for _, _, rows in segment)
    units, width = gate.shape
    blocks = 7

    def columns(rows):
        return pl.BlockSpec((rows, width // blocks), lambda i: (0, i))

    whole = pl.BlockSpec((units, height), lambda i: (0, 0))
    rows_shape = jax.ShapeDtypeStruct((height, width), jnp.bfloat16)
    return pl.pallas_call(
        functools.partial(forward_block, places, len(arrays)),
        grid=(blocks,),
        in_specs=[pl.BlockSpec(memory_space=pltpu.SMEM)]
        + [columns(v.shape[0]) for v in (*arrays, gate, rest)],
        out_specs=[columns(height)] * 2 + [whole] * 3,
        out_shape=[rows_shape] * 2 + [jax.ShapeDtypeStruct((units, height), jnp.bfloat16)] * 3,
        scratch_shapes=[pltpu.VMEM((units, height), jnp.float32)] * 3,
        compiler_params=pltpu.CompilerParams(vmem_limit_bytes=48 * 1024 * 1024),
        cost_estimate=pl.CostEstimate(
            flops=6 * units * height * width, bytes_accessed=10 * height * width, transcendentals=0
        ),
        name="forward",
    )(own_x.reshape(1), *arrays, gate, rest)


def weight_block(source_ref, rows_ref, out_ref):
    out_ref[...] = jnp.dot(
        source_ref[...], rows_ref[...], preferred_element_type=jnp.float32
    ).astype(jnp.bfloat16)


def weight_grads(source, rows):
    units, height = source.shape
    width = rows.shape[1]
    blocks = 4
    return pl.pallas_call(
        weight_block,
        grid=(blocks,),
        in_specs=[
            pl.BlockSpec((units, height), lambda i: (0, 0)),
            pl.BlockSpec((height, width // blocks), lambda i: (0, i)),
        ],
        out_specs=pl.BlockSpec((units, width // blocks), lambda i: (0, i)),
        out_shape=jax.ShapeDtypeStruct((units, width), jnp.bfloat16),
        compiler_params=pltpu.CompilerParams(vmem_limit_bytes=32 * 1024 * 1024),
        cost_estimate=pl.CostEstimate(
            flops=2 * units * height * width,
            bytes_accessed=2 * (units + height) * width,
            transcendentals=0,
        ),
        name="weight_grads",
    )(source, rows)


def ring_gather(value, axis):
    half = value.shape[0] // 2
    below = moved(value, **{axis: 1})
    above = moved(value, **{axis: -1})
    far_first = moved(below[:half], **{axis: 1})
    far_second = moved(above[half:], **{axis: -1})
    return [value, below, above, far_first, far_second]


def ring_scatter(part):
    rows = part.shape[0] // 4
    half = rows // 2

    def added(*terms):
        return sum(v.astype(jnp.float32) for v in terms).astype(jnp.bfloat16)

    via_above = moved(part[2 * rows : 2 * rows + half], dx=1)
    via_below = moved(part[2 * rows + half : 3 * rows], dx=-1)
    up_first = added(part[rows : rows + half], via_above)
    down_second = added(part[3 * rows + half :], via_below)
    below = moved(jnp.concatenate([up_first, part[rows + half : 2 * rows]], 0), dx=1)
    above = moved(jnp.concatenate([part[3 * rows : 3 * rows + half], down_second], 0), dx=-1)
    other = moved(added(part[half:rows], below[half:], above[half:]), dz=HALF_Z)
    return below, above, other


def adam_block(below_ref, above_ref, other_ref, own_ref, held_ref, one_ref, two_ref, *refs):
    new_held_ref, new_one_ref, new_two_ref, rollout_ref = refs[-4:]
    grads = own_ref[...].astype(jnp.float32)
    for ref in (below_ref, above_ref, other_ref):
        grads += ref[...].astype(jnp.float32)
    one = beta_one * one_ref[...] + (1.0 - beta_one) * grads
    two = beta_two * two_ref[...] + (1.0 - beta_two) * grads * grads
    correct_one = 1.0 - beta_one**step_count
    correct_two = 1.0 - beta_two**step_count
    update = one / correct_one / (jnp.sqrt(two / correct_two) + adam_eps)
    held = held_ref[...]
    held = held - adam_lr * (update + decay_rate * held)
    new_held_ref[...] = held
    new_one_ref[...] = one
    new_two_ref[...] = two
    rollout_ref[...] = held.astype(jnp.bfloat16)


def adam(part, below, above, other, own, held, one, two, done):
    rows, width = other.shape
    blocks = 2
    block = width // blocks
    here = pl.BlockSpec((rows, block), lambda i: (0, i))
    whole = pl.BlockSpec((rows, block), lambda i: (0, part * blocks + i))
    full = jax.ShapeDtypeStruct(held.shape, jnp.float32)
    return pl.pallas_call(
        adam_block,
        grid=(blocks,),
        in_specs=[here] * 4 + [whole] * 3 + [pl.BlockSpec(memory_space=pl.ANY)] * len(done),
        out_specs=[whole, whole, whole, here],
        out_shape=[full, full, full, jax.ShapeDtypeStruct((rows, width), jnp.bfloat16)],
        input_output_aliases={7 + i: i for i in range(len(done))},
        cost_estimate=pl.CostEstimate(flops=20 * rows * width, bytes_accessed=28 * rows * width, transcendentals=0),
        name="adam",
    )(below, above, other, own, held, one, two, *done)


def shards(
    tokens,
    routes,
    gate_scale,
    cotangent,
    master,
    moment_one,
    moment_two,
    dec_tokens,
    dec_routes,
    dec_scale,
):
    replicas = lax.axis_size("dp")
    groups = lax.axis_size("group")
    width = tokens.shape[1]
    own_group = lax.axis_index("group")
    own_expert = own_group % EXPERTS
    own_z, own_c = own_expert // NC, own_expert % NC

    per_peer = DCAP // NY
    steps, dec_dev = dec_tokens.shape[0], dec_tokens.shape[1]
    dec_ids = dec_routes[..., 0]
    dec_slot = rank_within(dec_ids, EXPERTS, 1)
    block = (dec_slot // per_peer + own_group) % NY
    target = block * EXPERTS + dec_ids
    dec_position = (target * steps + jnp.arange(steps, dtype=jnp.int32)[:, None]) * per_peer
    dec_position = (dec_position + dec_slot % per_peer).reshape(steps * dec_dev)
    dec_slots = groups * steps * per_peer
    dec_select = (
        jnp.arange(dec_slots, dtype=jnp.int32)[:, None] == dec_position[None, :]
    ).astype(jnp.bfloat16)
    dec_packed = jnp.dot(
        dec_select, dec_tokens.reshape(steps * dec_dev, width), preferred_element_type=jnp.float32
    ).astype(jnp.bfloat16)
    scaled = (gate_scale * cotangent.astype(jnp.float32)).astype(jnp.bfloat16)
    route_ids = routes[:, 0]
    slot = rank_within(route_ids, EXPERTS, 0)
    ahead = (route_ids // NC - own_z) % HALF_Z
    position = ahead * (2 * CAP) + slot
    same_core = route_ids % NC == own_c
    position_own = jnp.where(same_core, position, -1)
    position_other = moved(jnp.where(same_core, -1, position + CAP)[None], swap_core=True)[0]
    tokens_other = moved(tokens, swap_core=True)
    scaled_other = moved(scaled, swap_core=True)
    positions = jnp.concatenate([position_own, position_other])
    select = (
        jnp.arange(HALF_Z * 2 * CAP, dtype=jnp.int32)[:, None] == positions[None, :]
    ).astype(jnp.bfloat16)
    near, step_up, step_down, far_up, far_down = pack(
        CAP, select, tokens, tokens_other, scaled, scaled_other
    )
    span = 2 * CAP
    full = 2 * span

    master_rows = master[0]
    own = [
        master_rows[:, part * width : (part + 1) * width].astype(jnp.bfloat16) for part in range(3)
    ]
    u = own[0].shape[0]
    gate_z = moved(own[0], dz=HALF_Z)

    along_x = [[x * 2 + half for x in range(NX)] for half in range(2)]

    def over_x(value):
        return lax.all_gather(value, "dp", axis=0, tiled=True, axis_index_groups=along_x)

    near_below, near_above = moved(near, dy=1), moved(near, dy=-1)
    zb, za = moved(step_up, dz=1), moved(step_down, dz=-1)
    (gate_pair,) = assemble([[[(own[0], 0, u)], [(gate_z, 0, u)]]], [near])
    gate_weights = over_x(gate_pair)

    up, down, rest, far_up, far_down = assemble(
        [
            [[(near_below, 0, span)], [(zb, 0, full)], [(za, 0, full)]],
            [[(near_above, span, span)], [(zb, 0, full)], [(za, 0, full)]],
            [[(own[1], 0, u)], [(own[2], 0, u)]],
            [[(far_up, 0, span)]],
            [[(far_down, 0, span)]],
        ]
    )
    up2, down2 = moved(up, dy=1), moved(down, dy=-1)
    rest_z = moved(rest, dz=HALF_Z)
    zfb, zfa = moved(far_up, dz=2), moved(far_down, dz=-2)

    up, down, rest_pair, dec_packed = assemble(
        [
            [[(up2, span, span)], [(up2, span + full, span)], [(zfb, 0, span)], [(zfa, 0, span)]],
            [
                [(down2, 2 * span, span)],
                [(down2, 2 * span + full, span)],
                [(zfb, 0, span)],
                [(zfa, 0, span)],
            ],
            [[(own[1], 0, u)], [(rest_z, 0, u)], [(own[2], 0, u)], [(rest_z, u, u)]],
            [[(dec_packed, 0, dec_packed.shape[0])]],
        ]
    )
    up3, down3 = moved(up, dy=1), moved(down, dy=-1)
    rest_weights = over_x(rest_pair)
    dec_rows = lax.all_to_all(
        dec_packed.reshape(groups, steps * per_peer, width), "group", 0, 0, tiled=True
    ).reshape(dec_slots, width)

    up, down = assemble([[[(up3, 2 * span, span)]], [[(down3, 3 * span, span)]]], [dec_rows])
    up4, down4 = moved(up, dy=1), moved(down, dy=-1)

    def cuts(*places, rows=span):
        return [[(array, start, rows)] for array, start in places]

    x_recipe = cuts((near, 0), (near_below, 0), (near_above, 0), (up2, 0))
    d_recipe = cuts((near, span), (near_below, span), (near_above, span), (down2, 0))
    for i, held in enumerate((zb, za)):
        at = span + i * full
        x_recipe += cuts((held, 0), (up2, at), (down2, at), (up3, i * span))
        d_recipe += cuts((held, span), (up2, at + span), (down2, at + span), (down3, i * span))
    lasts = [(zfb, 0), (zfa, 0)]
    lasts += [(v, at) for v in (up3, down3) for at in (full, full + span)]
    lasts += [(up4, 0), (down4, 0)]
    for (one, at), (two, to) in zip(lasts[::2], lasts[1::2]):
        x_recipe.append([(one, at, CAP), (two, to, CAP)])
        d_recipe.append([(one, at + CAP, CAP), (two, to + CAP, CAP)])
    own_x = lax.axis_index("dp") // 2
    x_rows, d_rows, grad_gate, grad_up, activated = forward(
        x_recipe, d_recipe, gate_weights, rest_weights, own_x
    )
    parts = [
        weight_grads(grad_gate, x_rows),
        weight_grads(grad_up, x_rows),
        weight_grads(activated, d_rows),
    ]

    optimizer = (master_rows, moment_one[0], moment_two[0])
    done, rollout = [], []
    arrived = [ring_scatter(part) for part in parts]
    for part in range(3):
        *done, fresh = adam(part, *arrived[part], parts[part], *optimizer, done)
        rollout.append(jnp.concatenate(ring_gather(fresh, "dy"), 0))

    dec_gate = contract_rows(dec_rows, rollout[0])
    dec_up = contract_rows(dec_rows, rollout[1])
    dec_act = (silu_parts(dec_gate)[0] * dec_up).astype(jnp.bfloat16)
    partial = jnp.dot(dec_act, rollout[2], preferred_element_type=jnp.float32).astype(jnp.bfloat16)
    out_width = width // replicas
    padded = -(-out_width // 128) * 128
    depth = steps * per_peer
    partial = partial.reshape(groups, depth, replicas, out_width).transpose(0, 2, 1, 3)
    partial = jnp.pad(partial, ((0, 0), (0, 0), (0, 0), (0, padded - out_width)))
    partial = partial.reshape(groups * replicas, depth * padded // 128, 128)
    returned = lax.all_to_all(partial, ALL, 0, 0, tiled=True)
    returned = returned.reshape(groups, replicas, depth, padded).astype(jnp.float32)
    expert_out = jnp.sum(returned, 1)[..., :out_width].astype(jnp.bfloat16)
    expert_out = expert_out.reshape(dec_slots, out_width)
    picked = lax.dot_general(
        dec_select, expert_out, (((0,), (0,)), ((), ())), preferred_element_type=jnp.float32
    ).reshape(steps, dec_dev, out_width)
    dec_out = (dec_scale * picked).astype(jnp.bfloat16)
    return (*(value[None] for value in done), dec_out)


def solution(mesh):
    in_specs = (
        P(("group", "dp"), None),
        P(("group", "dp"), None),
        P(("group", "dp"), None),
        P(("group", "dp"), None),
        P("group", "dp", None),
        P("group", "dp", None),
        P("group", "dp", None),
        P(None, "group", None),
        P(None, "group", None),
        P(None, "group", None),
    )
    out_specs = (
        P("group", "dp", None),
        P("group", "dp", None),
        P("group", "dp", None),
        P(None, "group", "dp"),
    )
    return jax.shard_map(shards, mesh=mesh, in_specs=in_specs, out_specs=out_specs, check_vma=False)
```

```python
import functools

import jax
import jax.numpy as jnp
from jax import lax
from jax.experimental import pallas as pl
from jax.experimental.pallas import tpu as pltpu
from jax.sharding import PartitionSpec as P

EXPERTS = 8
CAP = 24
DCAP = 4
NY, NZ, NC, NX = 4, 8, 2, 4
HALF_Z = 4
ALL = ("group", "dp")

adam_lr = 0.001
beta_one = 0.9
beta_two = 0.95
adam_eps = 1e-08
decay_rate = 0.1
step_count = 100.0


def device_at(y, z, c, x):
    y, z, x = y % NY, z % NZ, x % NX
    group = (y * HALF_Z + z % HALF_Z) * NC + c
    return group * (NX * 2) + x * 2 + z // HALF_Z


def moved(value, dy=0, dz=0, swap_core=False, dx=0):
    pairs = []
    for y in range(NY):
        for z in range(NZ):
            for c in range(NC):
                for x in range(NX):
                    target = device_at(y + dy, z + dz, 1 - c if swap_core else c, x + dx)
                    pairs.append((device_at(y, z, c, x), target))
    return lax.ppermute(value, ALL, pairs)


def silu_parts(values):
    sig = jax.nn.sigmoid(values)
    return (values * sig, sig * (1.0 + values * (1.0 - sig)))


def rank_within(route_ids, experts, axis_dim):
    onehot = (route_ids[..., None] == jnp.arange(experts, dtype=jnp.int32)).astype(jnp.int32)
    running = jnp.cumsum(onehot, axis=axis_dim) - 1
    return jnp.sum(running * onehot, axis=-1)


def contract_rows(left, right):
    return lax.dot_general(
        left, right, (((1,), (1,)), ((), ())), preferred_element_type=jnp.float32
    )


def assemble(recipes, after=()):
    arrays, places = [], {}
    for recipe in recipes:
        for segment in recipe:
            for array, _, _ in segment:
                if id(array) not in places:
                    places[id(array)] = len(arrays)
                    arrays.append(array)
    heights = [sum(segment[0][2] for segment in recipe) for recipe in recipes]
    count = len(arrays) + len(after)
    width = arrays[0].shape[1]
    blocks = 2

    def columns(rows):
        return pl.BlockSpec((rows, width // blocks), lambda i: (0, i))

    def body(*refs):
        for out, recipe in enumerate(recipes):
            at = 0
            for segment in recipe:
                values = [refs[places[id(v)]][start : start + rows] for v, start, rows in segment]
                if len(values) > 1:
                    total = values[0].astype(jnp.float32)
                    for value in values[1:]:
                        total += value.astype(jnp.float32)
                    values = [total.astype(jnp.bfloat16)]
                rows = segment[0][2]
                refs[count + out][at : at + rows] = values[0]
                at += rows

    return pl.pallas_call(
        body,
        grid=(blocks,),
        in_specs=[columns(v.shape[0]) for v in arrays]
        + [pl.BlockSpec(memory_space=pl.ANY)] * len(after),
        out_specs=[columns(h) for h in heights],
        out_shape=[jax.ShapeDtypeStruct((h, width), jnp.bfloat16) for h in heights],
        cost_estimate=pl.CostEstimate(
            flops=0, bytes_accessed=4 * sum(heights) * width, transcendentals=0
        ),
        name="assemble",
    )(*arrays, *after)


def held_back(value, after):
    def body(*refs):
        del refs

    anywhere = pl.BlockSpec(memory_space=pl.ANY)
    return pl.pallas_call(
        body,
        in_specs=[anywhere] * (1 + len(after)),
        out_specs=anywhere,
        out_shape=jax.ShapeDtypeStruct(value.shape, value.dtype),
        input_output_aliases={0: 0},
        cost_estimate=pl.CostEstimate(flops=0, bytes_accessed=0, transcendentals=0),
        name="held_back",
    )(value, *after)


def pack_block(cap, select_ref, x_own, x_other, d_own, d_other, near, up, down, far_up, far_down):
    pairs = []
    for own, other in ((x_own, x_other), (d_own, d_other)):
        rows = jnp.concatenate([own[...], other[...]], 0)
        pairs.append(jnp.dot(select_ref[...], rows, preferred_element_type=jnp.float32))
    span = 2 * cap
    for out, at in ((near, 0), (up, 1), (down, 3)):
        out[:span] = pairs[0][at * span : (at + 1) * span].astype(jnp.bfloat16)
        out[span:] = pairs[1][at * span : (at + 1) * span].astype(jnp.bfloat16)
    for out, at in ((far_up, 2 * span), (far_down, 2 * span + cap)):
        out[...] = jnp.concatenate([v[at : at + cap] for v in pairs], 0).astype(jnp.bfloat16)


def pack(cap, select, *rows):
    width = rows[0].shape[1]
    blocks = 2
    block = width // blocks

    def columns(count):
        return pl.BlockSpec((count, block), lambda i: (0, i))

    heights = [4 * cap, 4 * cap, 4 * cap, 2 * cap, 2 * cap]
    return pl.pallas_call(
        functools.partial(pack_block, cap),
        grid=(blocks,),
        in_specs=[pl.BlockSpec(select.shape, lambda i: (0, 0))] + [columns(v.shape[0]) for v in rows],
        out_specs=[columns(h) for h in heights],
        out_shape=[jax.ShapeDtypeStruct((h, width), jnp.bfloat16) for h in heights],
        cost_estimate=pl.CostEstimate(
            flops=4 * select.size * width, bytes_accessed=2 * (4 * 128 + sum(heights)) * width, transcendentals=0
        ),
        name="pack",
    )(select, *rows)


def forward_block(places, count, own_x_ref, *refs):
    pieces, gate_ref, rest_ref = refs[:count], refs[count], refs[count + 1]
    outs, sums = refs[count + 2 : -3], refs[-3:]
    step = pl.program_id(0)
    for out, recipe in zip(outs[:2], places):
        at = 0
        for segment in recipe:
            values = [pieces[i][start : start + rows] for i, start, rows in segment]
            if len(values) > 1:
                values = [v.astype(jnp.float32) for v in values]
                values = [jnp.concatenate(values, 0).astype(jnp.bfloat16)]
            out[at : at + values[0].shape[0]] = values[0]
            at += values[0].shape[0]
    unit = rest_ref.shape[0] // (2 * NX)
    parts = [gate_ref[...]]
    for i in range(2):
        cuts = [rest_ref[(2 * x + i) * unit : (2 * x + i + 1) * unit] for x in range(NX)]
        parts.append(jnp.concatenate(cuts, 0))
    for total, part, rows in zip(sums, parts, (outs[0], outs[0], outs[1])):
        product = contract_rows(part, rows[...])

        @pl.when(step == 0)
        def _():
            total[...] = product

        @pl.when(step > 0)
        def _():
            total[...] += product

    @pl.when(step == pl.num_programs(0) - 1)
    def _():
        for x in range(NX):
            cut = slice(x * unit, (x + 1) * unit)
            gate_pre, up_pre, back_pre = (total[cut] for total in sums)
            silu_val, silu_grad = silu_parts(gate_pre)
            ahead = (x - own_x_ref[0] + NX) % NX
            to = pl.ds(pl.multiple_of(ahead * unit, unit), unit)
            outs[2][to] = (back_pre * up_pre * silu_grad).astype(jnp.bfloat16)
            outs[3][to] = (back_pre * silu_val).astype(jnp.bfloat16)
            outs[4][to] = (silu_val * up_pre).astype(jnp.bfloat16)


def forward(x_recipe, d_recipe, gate, rest, own_x):
    arrays, index = [], {}
    for recipe in (x_recipe, d_recipe):
        for segment in recipe:
            for array, _, _ in segment:
                if id(array) not in index:
                    index[id(array)] = len(arrays)
                    arrays.append(array)
    places = [
        [[(index[id(v)], start, rows) for v, start, rows in segment] for segment in recipe]
        for recipe in (x_recipe, d_recipe)
    ]
    height = sum(rows for segment in x_recipe for _, _, rows in segment)
    units, width = gate.shape
    blocks = 2

    def columns(rows):
        return pl.BlockSpec((rows, width // blocks), lambda i: (0, i))

    whole = pl.BlockSpec((units, height), lambda i: (0, 0))
    rows_shape = jax.ShapeDtypeStruct((height, width), jnp.bfloat16)
    return pl.pallas_call(
        functools.partial(forward_block, places, len(arrays)),
        grid=(blocks,),
        in_specs=[pl.BlockSpec(memory_space=pltpu.SMEM)]
        + [columns(v.shape[0]) for v in (*arrays, gate, rest)],
        out_specs=[columns(height)] * 2 + [whole] * 3,
        out_shape=[rows_shape] * 2 + [jax.ShapeDtypeStruct((units, height), jnp.bfloat16)] * 3,
        scratch_shapes=[pltpu.VMEM((units, height), jnp.float32)] * 3,
        compiler_params=pltpu.CompilerParams(vmem_limit_bytes=60 * 1024 * 1024),
        cost_estimate=pl.CostEstimate(
            flops=6 * units * height * width, bytes_accessed=10 * height * width, transcendentals=0
        ),
        name="forward",
    )(own_x.reshape(1), *arrays, gate, rest)


def weight_block(source_ref, rows_ref, out_ref):
    out_ref[...] = jnp.dot(
        source_ref[...], rows_ref[...], preferred_element_type=jnp.float32
    ).astype(jnp.bfloat16)


def weight_grads(source, rows):
    units, height = source.shape
    width = rows.shape[1]
    blocks = 1
    return pl.pallas_call(
        weight_block,
        grid=(blocks,),
        in_specs=[
            pl.BlockSpec((units, height), lambda i: (0, 0)),
            pl.BlockSpec((height, width // blocks), lambda i: (0, i)),
        ],
        out_specs=pl.BlockSpec((units, width // blocks), lambda i: (0, i)),
        out_shape=jax.ShapeDtypeStruct((units, width), jnp.bfloat16),
        compiler_params=pltpu.CompilerParams(vmem_limit_bytes=32 * 1024 * 1024),
        cost_estimate=pl.CostEstimate(
            flops=2 * units * height * width,
            bytes_accessed=2 * (units + height) * width,
            transcendentals=0,
        ),
        name="weight_grads",
    )(source, rows)


def ring_gather(value, axis):
    half = value.shape[0] // 2
    below = moved(value, **{axis: 1})
    above = moved(value, **{axis: -1})
    far_first = moved(below[:half], **{axis: 1})
    far_second = moved(above[half:], **{axis: -1})
    return [value, below, above, far_first, far_second]


def ring_scatter(part):
    rows = part.shape[0] // 4
    half = rows // 2

    def added(*terms):
        return sum(v.astype(jnp.float32) for v in terms).astype(jnp.bfloat16)

    via_above = moved(part[2 * rows : 2 * rows + half], dx=1)
    via_below = moved(part[2 * rows + half : 3 * rows], dx=-1)
    up_first = added(part[rows : rows + half], via_above)
    down_second = added(part[3 * rows + half :], via_below)
    below = moved(jnp.concatenate([up_first, part[rows + half : 2 * rows]], 0), dx=1)
    above = moved(jnp.concatenate([part[3 * rows : 3 * rows + half], down_second], 0), dx=-1)
    other = moved(added(part[half:rows], below[half:], above[half:]), dz=HALF_Z)
    return below, above, other


def adam_block(below_ref, above_ref, other_ref, own_ref, held_ref, one_ref, two_ref, *refs):
    new_held_ref, new_one_ref, new_two_ref, rollout_ref = refs[-4:]
    grads = own_ref[...].astype(jnp.float32)
    for ref in (below_ref, above_ref, other_ref):
        grads += ref[...].astype(jnp.float32)
    one = beta_one * one_ref[...] + (1.0 - beta_one) * grads
    two = beta_two * two_ref[...] + (1.0 - beta_two) * grads * grads
    correct_one = 1.0 - beta_one**step_count
    correct_two = 1.0 - beta_two**step_count
    update = one / correct_one / (jnp.sqrt(two / correct_two) + adam_eps)
    held = held_ref[...]
    held = held - adam_lr * (update + decay_rate * held)
    new_held_ref[...] = held
    new_one_ref[...] = one
    new_two_ref[...] = two
    rollout_ref[...] = held.astype(jnp.bfloat16)


def adam(part, below, above, other, own, held, one, two, done, after):
    rows, width = other.shape
    blocks = 1
    block = width // blocks
    here = pl.BlockSpec((rows, block), lambda i: (0, i))
    whole = pl.BlockSpec((rows, block), lambda i: (0, part * blocks + i))
    full = jax.ShapeDtypeStruct(held.shape, jnp.float32)
    return pl.pallas_call(
        adam_block,
        grid=(blocks,),
        in_specs=[here] * 4 + [whole] * 3 + [pl.BlockSpec(memory_space=pl.ANY)] * (len(done) + len(after)),
        out_specs=[whole, whole, whole, here],
        out_shape=[full, full, full, jax.ShapeDtypeStruct((rows, width), jnp.bfloat16)],
        compiler_params=pltpu.CompilerParams(vmem_limit_bytes=32 * 1024 * 1024),
        input_output_aliases={7 + i: i for i in range(len(done))},
        cost_estimate=pl.CostEstimate(flops=20 * rows * width, bytes_accessed=28 * rows * width, transcendentals=0),
        name="adam",
    )(below, above, other, own, held, one, two, *done, *after)


def shards(
    tokens,
    routes,
    gate_scale,
    cotangent,
    master,
    moment_one,
    moment_two,
    dec_tokens,
    dec_routes,
    dec_scale,
):
    replicas = lax.axis_size("dp")
    groups = lax.axis_size("group")
    width = tokens.shape[1]
    own_group = lax.axis_index("group")
    own_expert = own_group % EXPERTS
    own_z, own_c = own_expert // NC, own_expert % NC

    per_peer = DCAP // NY
    steps, dec_dev = dec_tokens.shape[0], dec_tokens.shape[1]
    dec_ids = dec_routes[..., 0]
    dec_slot = rank_within(dec_ids, EXPERTS, 1)
    block = (dec_slot // per_peer + own_group) % NY
    target = block * EXPERTS + dec_ids
    depth = steps * per_peer
    dec_slots = groups * depth
    dec_step = jnp.arange(steps, dtype=jnp.int32)[:, None]
    dec_place = dec_step * per_peer + dec_slot % per_peer
    dec_position = (target * depth + dec_place).reshape(steps * dec_dev)
    dec_select = (
        jnp.arange(dec_slots, dtype=jnp.int32)[:, None] == dec_position[None, :]
    ).astype(jnp.bfloat16)
    half_position = (target * 2 * depth + dec_place).reshape(steps * dec_dev)
    half_select = (
        jnp.arange(2 * dec_slots, dtype=jnp.int32)[:, None]
        == jnp.concatenate([half_position, half_position + depth])[None, :]
    ).astype(jnp.bfloat16)
    dec_flat = dec_tokens.reshape(steps * dec_dev, width)
    dec_packed = jnp.dot(
        half_select,
        jnp.concatenate([dec_flat[:, : width // 2], dec_flat[:, width // 2 :]], 0),
        preferred_element_type=jnp.float32,
    ).astype(jnp.bfloat16)

    scaled = (gate_scale * cotangent.astype(jnp.float32)).astype(jnp.bfloat16)
    route_ids = routes[:, 0]
    slot = rank_within(route_ids, EXPERTS, 0)
    ahead = (route_ids // NC - own_z) % HALF_Z
    position = ahead * (2 * CAP) + slot
    same_core = route_ids % NC == own_c
    position_own = jnp.where(same_core, position, -1)
    position_other = moved(jnp.where(same_core, -1, position + CAP)[None], swap_core=True)[0]
    tokens_other = moved(tokens, swap_core=True)
    scaled_other = moved(scaled, swap_core=True)
    positions = jnp.concatenate([position_own, position_other])
    select = (
        jnp.arange(HALF_Z * 2 * CAP, dtype=jnp.int32)[:, None] == positions[None, :]
    ).astype(jnp.bfloat16)
    near, step_up, step_down, far_up, far_down = pack(
        CAP, select, tokens, tokens_other, scaled, scaled_other
    )
    span = 2 * CAP
    full = 2 * span

    master_rows = master[0]
    own = [
        master_rows[:, part * width : (part + 1) * width].astype(jnp.bfloat16) for part in range(3)
    ]
    u = own[0].shape[0]
    gate_z = moved(own[0], dz=HALF_Z)

    along_x = [[x * 2 + half for x in range(NX)] for half in range(2)]

    def over_x(value):
        return lax.all_gather(value, "dp", axis=0, tiled=True, axis_index_groups=along_x)

    near_below, near_above = moved(near, dy=1), moved(near, dy=-1)
    zb, za = moved(step_up, dz=1), moved(step_down, dz=-1)
    (gate_pair,) = assemble([[[(own[0], 0, u)], [(gate_z, 0, u)]]], [near])
    gate_weights = over_x(gate_pair)

    up, down, rest, far_up, far_down = assemble(
        [
            [[(near_below, 0, span)], [(zb, 0, full)], [(za, 0, full)]],
            [[(near_above, span, span)], [(zb, 0, full)], [(za, 0, full)]],
            [[(own[1], 0, u)], [(own[2], 0, u)]],
            [[(far_up, 0, span)]],
            [[(far_down, 0, span)]],
        ]
    )
    up2, down2 = moved(up, dy=1), moved(down, dy=-1)
    rest_z = moved(rest, dz=HALF_Z)
    zfb, zfa = moved(far_up, dz=2), moved(far_down, dz=-2)

    up, down, rest_pair = assemble(
        [
            [[(up2, span, span)], [(up2, span + full, span)], [(zfb, 0, span)], [(zfa, 0, span)]],
            [
                [(down2, 2 * span, span)],
                [(down2, 2 * span + full, span)],
                [(zfb, 0, span)],
                [(zfa, 0, span)],
            ],
            [[(own[1], 0, u)], [(rest_z, 0, u)], [(own[2], 0, u)], [(rest_z, u, u)]],
        ]
    )
    up3, down3 = moved(up, dy=1), moved(down, dy=-1)
    rest_weights = over_x(rest_pair)
    up, down = assemble([[[(up3, 2 * span, span)]], [[(down3, 3 * span, span)]]])
    up4, down4 = moved(up, dy=1), moved(down, dy=-1)
    def cuts(*places, rows=span):
        return [[(array, start, rows)] for array, start in places]

    x_recipe = cuts((near, 0), (near_below, 0), (near_above, 0), (up2, 0))
    d_recipe = cuts((near, span), (near_below, span), (near_above, span), (down2, 0))
    for i, held in enumerate((zb, za)):
        at = span + i * full
        x_recipe += cuts((held, 0), (up2, at), (down2, at), (up3, i * span))
        d_recipe += cuts((held, span), (up2, at + span), (down2, at + span), (down3, i * span))
    lasts = [(zfb, 0), (zfa, 0)]
    lasts += [(v, at) for v in (up3, down3) for at in (full, full + span)]
    lasts += [(up4, 0), (down4, 0)]
    for (one, at), (two, to) in zip(lasts[::2], lasts[1::2]):
        x_recipe.append([(one, at, CAP), (two, to, CAP)])
        d_recipe.append([(one, at + CAP, CAP), (two, to + CAP, CAP)])
    own_x = lax.axis_index("dp") // 2
    x_rows, d_rows, grad_gate, grad_up, activated = forward(
        x_recipe, d_recipe, gate_weights, rest_weights, own_x
    )
    parts = [
        weight_grads(grad_gate, x_rows),
        weight_grads(grad_up, x_rows),
        weight_grads(activated, d_rows),
    ]

    optimizer = (master_rows, moment_one[0], moment_two[0])
    arrived = [ring_scatter(part) for part in parts]
    dec_packed = held_back(dec_packed, [up4, down4])
    dec_rows = lax.all_to_all(
        dec_packed.reshape(groups, 2 * depth, width // 2), "group", 0, 0, tiled=True
    )
    done, fresh, after = [], [], []
    for part in range(3):
        if part == 1:
            dec_rows = held_back(dec_rows, fresh)
        if part == 2:
            gate_up = ring_gather(jnp.concatenate(fresh, 0), "dy")
            after = gate_up[1:3]
        *done, now = adam(part, *arrived[part], parts[part], *optimizer, done, after)
        fresh.append(now)
    held, below, above, far_gate, far_up = gate_up
    rollout = [
        jnp.concatenate([held[:u], below[:u], above[:u], far_gate], 0),
        jnp.concatenate([held[u:], below[u:], above[u:], far_up], 0),
        jnp.concatenate(ring_gather(fresh[2], "dy"), 0),
    ]

    dec_rows = dec_rows.reshape(2 * dec_slots, width // 2)

    def both_halves(units):
        first, second = (
            contract_rows(dec_rows, units[:, at * (width // 2) : (at + 1) * (width // 2)]).reshape(
                groups, 2, depth, -1
            )[:, at]
            for at in range(2)
        )
        return (first + second).reshape(dec_slots, -1)

    dec_gate, dec_up = both_halves(rollout[0]), both_halves(rollout[1])
    dec_act = (silu_parts(dec_gate)[0] * dec_up).astype(jnp.bfloat16)
    partial = jnp.dot(dec_act, rollout[2], preferred_element_type=jnp.float32).astype(jnp.bfloat16)
    out_width = width // replicas
    padded = -(-out_width // 128) * 128
    partial = partial.reshape(groups, depth, replicas, out_width).transpose(0, 2, 1, 3)
    partial = jnp.pad(partial, ((0, 0), (0, 0), (0, 0), (0, padded - out_width)))
    partial = partial.reshape(groups * replicas, depth * padded // 128, 128)
    returned = lax.all_to_all(partial, ALL, 0, 0, tiled=True)
    returned = returned.reshape(groups, replicas, depth, padded).astype(jnp.float32)
    expert_out = jnp.sum(returned, 1)[..., :out_width].astype(jnp.bfloat16)
    expert_out = expert_out.reshape(dec_slots, out_width)
    picked = lax.dot_general(
        dec_select, expert_out, (((0,), (0,)), ((), ())), preferred_element_type=jnp.float32
    ).reshape(steps, dec_dev, out_width)
    dec_out = (dec_scale * picked).astype(jnp.bfloat16)
    return (*(value[None] for value in done), dec_out)


def solution(mesh):
    in_specs = (
        P(("group", "dp"), None),
        P(("group", "dp"), None),
        P(("group", "dp"), None),
        P(("group", "dp"), None),
        P("group", "dp", None),
        P("group", "dp", None),
        P("group", "dp", None),
        P(None, "group", None),
        P(None, "group", None),
        P(None, "group", None),
    )
    out_specs = (
        P("group", "dp", None),
        P("group", "dp", None),
        P("group", "dp", None),
        P(None, "group", "dp"),
    )
    return jax.shard_map(shards, mesh=mesh, in_specs=in_specs, out_specs=out_specs, check_vma=False)
```

```python
import functools

import jax
import jax.numpy as jnp
from jax import lax
from jax.experimental import pallas as pl
from jax.experimental.pallas import tpu as pltpu
from jax.sharding import PartitionSpec as P

EXPERTS = 8
CAP = 24
DCAP = 4
NY, NZ, NC, NX = 4, 8, 2, 4
HALF_Z = 4
ALL = ("group", "dp")

adam_lr = 0.001
beta_one = 0.9
beta_two = 0.95
adam_eps = 1e-08
decay_rate = 0.1
step_count = 100.0


def device_at(y, z, c, x):
    y, z, x = y % NY, z % NZ, x % NX
    group = (y * HALF_Z + z % HALF_Z) * NC + c
    return group * (NX * 2) + x * 2 + z // HALF_Z


def moved(value, dy=0, dz=0, swap_core=False, dx=0):
    pairs = []
    for y in range(NY):
        for z in range(NZ):
            for c in range(NC):
                for x in range(NX):
                    target = device_at(y + dy, z + dz, 1 - c if swap_core else c, x + dx)
                    pairs.append((device_at(y, z, c, x), target))
    return lax.ppermute(value, ALL, pairs)


def silu_parts(values):
    sig = jax.nn.sigmoid(values)
    return (values * sig, sig * (1.0 + values * (1.0 - sig)))


def rank_within(route_ids, experts, axis_dim):
    onehot = (route_ids[..., None] == jnp.arange(experts, dtype=jnp.int32)).astype(jnp.int32)
    running = jnp.cumsum(onehot, axis=axis_dim) - 1
    return jnp.sum(running * onehot, axis=-1)


def contract_rows(left, right):
    return lax.dot_general(
        left, right, (((1,), (1,)), ((), ())), preferred_element_type=jnp.float32
    )


def assemble(recipes, after=()):
    arrays, places = [], {}
    for recipe in recipes:
        for segment in recipe:
            for array, _, _ in segment:
                if id(array) not in places:
                    places[id(array)] = len(arrays)
                    arrays.append(array)
    heights = [sum(segment[0][2] for segment in recipe) for recipe in recipes]
    count = len(arrays) + len(after)
    width = arrays[0].shape[1]
    blocks = 2

    def columns(rows):
        return pl.BlockSpec((rows, width // blocks), lambda i: (0, i))

    def body(*refs):
        for out, recipe in enumerate(recipes):
            at = 0
            for segment in recipe:
                values = [refs[places[id(v)]][start : start + rows] for v, start, rows in segment]
                if len(values) > 1:
                    total = values[0].astype(jnp.float32)
                    for value in values[1:]:
                        total += value.astype(jnp.float32)
                    values = [total.astype(jnp.bfloat16)]
                rows = segment[0][2]
                refs[count + out][at : at + rows] = values[0]
                at += rows

    return pl.pallas_call(
        body,
        grid=(blocks,),
        in_specs=[columns(v.shape[0]) for v in arrays]
        + [pl.BlockSpec(memory_space=pl.ANY)] * len(after),
        out_specs=[columns(h) for h in heights],
        out_shape=[jax.ShapeDtypeStruct((h, width), jnp.bfloat16) for h in heights],
        cost_estimate=pl.CostEstimate(
            flops=0, bytes_accessed=4 * sum(heights) * width, transcendentals=0
        ),
        name="assemble",
    )(*arrays, *after)


def held_back(value, after):
    def body(*refs):
        del refs

    anywhere = pl.BlockSpec(memory_space=pl.ANY)
    return pl.pallas_call(
        body,
        in_specs=[anywhere] * (1 + len(after)),
        out_specs=anywhere,
        out_shape=jax.ShapeDtypeStruct(value.shape, value.dtype),
        input_output_aliases={0: 0},
        cost_estimate=pl.CostEstimate(flops=0, bytes_accessed=0, transcendentals=0),
        name="held_back",
    )(value, *after)


def pack_block(cap, select_ref, x_own, x_other, d_own, d_other, near, up, down, far_up, far_down):
    pairs = []
    for own, other in ((x_own, x_other), (d_own, d_other)):
        rows = jnp.concatenate([own[...], other[...]], 0)
        pairs.append(jnp.dot(select_ref[...], rows, preferred_element_type=jnp.float32))
    span = 2 * cap
    for out, at in ((near, 0), (up, 1), (down, 3)):
        out[:span] = pairs[0][at * span : (at + 1) * span].astype(jnp.bfloat16)
        out[span:] = pairs[1][at * span : (at + 1) * span].astype(jnp.bfloat16)
    for out, at in ((far_up, 2 * span), (far_down, 2 * span + cap)):
        out[...] = jnp.concatenate([v[at : at + cap] for v in pairs], 0).astype(jnp.bfloat16)


def pack(cap, select, *rows):
    width = rows[0].shape[1]
    blocks = 2
    block = width // blocks

    def columns(count):
        return pl.BlockSpec((count, block), lambda i: (0, i))

    heights = [4 * cap, 4 * cap, 4 * cap, 2 * cap, 2 * cap]
    return pl.pallas_call(
        functools.partial(pack_block, cap),
        grid=(blocks,),
        in_specs=[pl.BlockSpec(select.shape, lambda i: (0, 0))] + [columns(v.shape[0]) for v in rows],
        out_specs=[columns(h) for h in heights],
        out_shape=[jax.ShapeDtypeStruct((h, width), jnp.bfloat16) for h in heights],
        cost_estimate=pl.CostEstimate(
            flops=4 * select.size * width, bytes_accessed=2 * (4 * 128 + sum(heights)) * width, transcendentals=0
        ),
        name="pack",
    )(select, *rows)


def forward_block(places, count, own_x_ref, *refs):
    pieces, gate_ref, rest_ref = refs[:count], refs[count], refs[count + 1]
    outs, sums = refs[count + 2 : -3], refs[-3:]
    step = pl.program_id(0)
    for out, recipe in zip(outs[:2], places):
        at = 0
        for segment in recipe:
            values = [pieces[i][start : start + rows] for i, start, rows in segment]
            if len(values) > 1:
                values = [v.astype(jnp.float32) for v in values]
                values = [jnp.concatenate(values, 0).astype(jnp.bfloat16)]
            out[at : at + values[0].shape[0]] = values[0]
            at += values[0].shape[0]
    unit = rest_ref.shape[0] // (2 * NX)
    parts = [gate_ref[...]]
    for i in range(2):
        cuts = [rest_ref[(2 * x + i) * unit : (2 * x + i + 1) * unit] for x in range(NX)]
        parts.append(jnp.concatenate(cuts, 0))
    for total, part, rows in zip(sums, parts, (outs[0], outs[0], outs[1])):
        product = contract_rows(part, rows[...])

        @pl.when(step == 0)
        def _():
            total[...] = product

        @pl.when(step > 0)
        def _():
            total[...] += product

    @pl.when(step == pl.num_programs(0) - 1)
    def _():
        for x in range(NX):
            cut = slice(x * unit, (x + 1) * unit)
            gate_pre, up_pre, back_pre = (total[cut] for total in sums)
            silu_val, silu_grad = silu_parts(gate_pre)
            ahead = (x - own_x_ref[0] + NX) % NX
            to = pl.ds(pl.multiple_of(ahead * unit, unit), unit)
            outs[2][to] = (back_pre * up_pre * silu_grad).astype(jnp.bfloat16)
            outs[3][to] = (back_pre * silu_val).astype(jnp.bfloat16)
            outs[4][to] = (silu_val * up_pre).astype(jnp.bfloat16)


def forward(x_recipe, d_recipe, gate, rest, own_x):
    arrays, index = [], {}
    for recipe in (x_recipe, d_recipe):
        for segment in recipe:
            for array, _, _ in segment:
                if id(array) not in index:
                    index[id(array)] = len(arrays)
                    arrays.append(array)
    places = [
        [[(index[id(v)], start, rows) for v, start, rows in segment] for segment in recipe]
        for recipe in (x_recipe, d_recipe)
    ]
    height = sum(rows for segment in x_recipe for _, _, rows in segment)
    units, width = gate.shape
    blocks = 2

    def columns(rows):
        return pl.BlockSpec((rows, width // blocks), lambda i: (0, i))

    whole = pl.BlockSpec((units, height), lambda i: (0, 0))
    rows_shape = jax.ShapeDtypeStruct((height, width), jnp.bfloat16)
    return pl.pallas_call(
        functools.partial(forward_block, places, len(arrays)),
        grid=(blocks,),
        in_specs=[pl.BlockSpec(memory_space=pltpu.SMEM)]
        + [columns(v.shape[0]) for v in (*arrays, gate, rest)],
        out_specs=[columns(height)] * 2 + [whole] * 3,
        out_shape=[rows_shape] * 2 + [jax.ShapeDtypeStruct((units, height), jnp.bfloat16)] * 3,
        scratch_shapes=[pltpu.VMEM((units, height), jnp.float32)] * 3,
        compiler_params=pltpu.CompilerParams(vmem_limit_bytes=60 * 1024 * 1024),
        cost_estimate=pl.CostEstimate(
            flops=6 * units * height * width, bytes_accessed=10 * height * width, transcendentals=0
        ),
        name="forward",
    )(own_x.reshape(1), *arrays, gate, rest)


def weight_block(source_ref, rows_ref, out_ref):
    out_ref[...] = jnp.dot(
        source_ref[...], rows_ref[...], preferred_element_type=jnp.float32
    ).astype(jnp.bfloat16)


def weight_grads(source, rows):
    units, height = source.shape
    width = rows.shape[1]
    blocks = 1
    return pl.pallas_call(
        weight_block,
        grid=(blocks,),
        in_specs=[
            pl.BlockSpec((units, height), lambda i: (0, 0)),
            pl.BlockSpec((height, width // blocks), lambda i: (0, i)),
        ],
        out_specs=pl.BlockSpec((units, width // blocks), lambda i: (0, i)),
        out_shape=jax.ShapeDtypeStruct((units, width), jnp.bfloat16),
        compiler_params=pltpu.CompilerParams(vmem_limit_bytes=32 * 1024 * 1024),
        cost_estimate=pl.CostEstimate(
            flops=2 * units * height * width,
            bytes_accessed=2 * (units + height) * width,
            transcendentals=0,
        ),
        name="weight_grads",
    )(source, rows)


def ring_gather(value, axis):
    half = value.shape[0] // 2
    below = moved(value, **{axis: 1})
    above = moved(value, **{axis: -1})
    far_first = moved(below[:half], **{axis: 1})
    far_second = moved(above[half:], **{axis: -1})
    return [value, below, above, far_first, far_second]


def ring_scatter(part):
    rows = part.shape[0] // 4
    half = rows // 2

    def added(*terms):
        return sum(v.astype(jnp.float32) for v in terms).astype(jnp.bfloat16)

    via_above = moved(part[2 * rows : 2 * rows + half], dx=1)
    via_below = moved(part[2 * rows + half : 3 * rows], dx=-1)
    up_first = added(part[rows : rows + half], via_above)
    down_second = added(part[3 * rows + half :], via_below)
    below = moved(jnp.concatenate([up_first, part[rows + half : 2 * rows]], 0), dx=1)
    above = moved(jnp.concatenate([part[3 * rows : 3 * rows + half], down_second], 0), dx=-1)
    other = moved(added(part[half:rows], below[half:], above[half:]), dz=HALF_Z)
    return below, above, other


def adam_block(count, *refs):
    held_ref, one_ref, two_ref = refs[4 * count : 4 * count + 3]
    new_held_ref, new_one_ref, new_two_ref, rollout_ref = refs[-4:]
    rows = rollout_ref.shape[0]

    def update(terms):
        grads = sum(ref[:rows].astype(jnp.float32) for ref in terms)
        one = beta_one * one_ref[...] + (1.0 - beta_one) * grads
        two = beta_two * two_ref[...] + (1.0 - beta_two) * grads * grads
        correct_one = 1.0 - beta_one**step_count
        correct_two = 1.0 - beta_two**step_count
        change = one / correct_one / (jnp.sqrt(two / correct_two) + adam_eps)
        held = held_ref[...]
        held = held - adam_lr * (change + decay_rate * held)
        new_held_ref[...] = held
        new_one_ref[...] = one
        new_two_ref[...] = two
        rollout_ref[...] = held.astype(jnp.bfloat16)

    for i in range(count):
        terms = refs[4 * i : 4 * i + 4]
        if count == 1:
            update(terms)
        else:
            pl.when(pl.program_id(0) == i)(functools.partial(update, terms))


def adam(first, terms, held, one, two, done, after):
    rows, width = held.shape[0], terms[0][0].shape[1]
    flat = [v for four in terms for v in four]
    ours = pl.BlockSpec((rows, width), lambda i: (0, first + i))
    full = jax.ShapeDtypeStruct(held.shape, jnp.float32)
    kept = len(flat) + 3
    return pl.pallas_call(
        functools.partial(adam_block, len(terms)),
        grid=(len(terms),),
        in_specs=[pl.BlockSpec((rows, width), lambda i: (0, 0))] * len(flat)
        + [ours] * 3
        + [pl.BlockSpec(memory_space=pl.ANY)] * (len(done) + len(after)),
        out_specs=[ours] * 3 + [pl.BlockSpec((rows, width), lambda i: (i, 0))],
        out_shape=[full] * 3 + [jax.ShapeDtypeStruct((len(terms) * rows, width), jnp.bfloat16)],
        input_output_aliases={kept + i: i for i in range(len(done))},
        compiler_params=pltpu.CompilerParams(vmem_limit_bytes=60 * 1024 * 1024),
        cost_estimate=pl.CostEstimate(
            flops=20 * len(terms) * rows * width,
            bytes_accessed=32 * len(terms) * rows * width,
            transcendentals=0,
        ),
        name="adam",
    )(*flat, held, one, two, *done, *after)


def shards(
    tokens,
    routes,
    gate_scale,
    cotangent,
    master,
    moment_one,
    moment_two,
    dec_tokens,
    dec_routes,
    dec_scale,
):
    replicas = lax.axis_size("dp")
    groups = lax.axis_size("group")
    width = tokens.shape[1]
    own_group = lax.axis_index("group")
    own_expert = own_group % EXPERTS
    own_z, own_c = own_expert // NC, own_expert % NC

    per_peer = DCAP // NY
    steps, dec_dev = dec_tokens.shape[0], dec_tokens.shape[1]
    dec_ids = dec_routes[..., 0]
    dec_slot = rank_within(dec_ids, EXPERTS, 1)
    block = (dec_slot // per_peer + own_group) % NY
    target = block * EXPERTS + dec_ids
    depth = steps * per_peer
    dec_slots = groups * depth
    dec_step = jnp.arange(steps, dtype=jnp.int32)[:, None]
    dec_place = dec_step * per_peer + dec_slot % per_peer
    dec_position = (target * depth + dec_place).reshape(steps * dec_dev)
    dec_select = (
        jnp.arange(dec_slots, dtype=jnp.int32)[:, None] == dec_position[None, :]
    ).astype(jnp.bfloat16)
    half_position = (target * 2 * depth + dec_place).reshape(steps * dec_dev)
    half_select = (
        jnp.arange(2 * dec_slots, dtype=jnp.int32)[:, None]
        == jnp.concatenate([half_position, half_position + depth])[None, :]
    ).astype(jnp.bfloat16)
    dec_flat = dec_tokens.reshape(steps * dec_dev, width)
    dec_packed = jnp.dot(
        half_select,
        jnp.concatenate([dec_flat[:, : width // 2], dec_flat[:, width // 2 :]], 0),
        preferred_element_type=jnp.float32,
    ).astype(jnp.bfloat16)

    scaled = (gate_scale * cotangent.astype(jnp.float32)).astype(jnp.bfloat16)
    route_ids = routes[:, 0]
    slot = rank_within(route_ids, EXPERTS, 0)
    ahead = (route_ids // NC - own_z) % HALF_Z
    position = ahead * (2 * CAP) + slot
    same_core = route_ids % NC == own_c
    position_own = jnp.where(same_core, position, -1)
    position_other = moved(jnp.where(same_core, -1, position + CAP)[None], swap_core=True)[0]
    tokens_other = moved(tokens, swap_core=True)
    scaled_other = moved(scaled, swap_core=True)
    positions = jnp.concatenate([position_own, position_other])
    select = (
        jnp.arange(HALF_Z * 2 * CAP, dtype=jnp.int32)[:, None] == positions[None, :]
    ).astype(jnp.bfloat16)
    near, step_up, step_down, far_up, far_down = pack(
        CAP, select, tokens, tokens_other, scaled, scaled_other
    )
    span = 2 * CAP
    full = 2 * span

    master_rows = master[0]
    own = [
        master_rows[:, part * width : (part + 1) * width].astype(jnp.bfloat16) for part in range(3)
    ]
    u = own[0].shape[0]
    gate_z = moved(own[0], dz=HALF_Z)

    along_x = [[x * 2 + half for x in range(NX)] for half in range(2)]

    def over_x(value):
        return lax.all_gather(value, "dp", axis=0, tiled=True, axis_index_groups=along_x)

    near_below, near_above = moved(near, dy=1), moved(near, dy=-1)
    zb, za = moved(step_up, dz=1), moved(step_down, dz=-1)
    (gate_pair,) = assemble([[[(own[0], 0, u)], [(gate_z, 0, u)]]], [near])
    gate_weights = over_x(gate_pair)

    up, down, rest, far_up, far_down = assemble(
        [
            [[(near_below, 0, span)], [(zb, 0, full)], [(za, 0, full)]],
            [[(near_above, span, span)], [(zb, 0, full)], [(za, 0, full)]],
            [[(own[1], 0, u)], [(own[2], 0, u)]],
            [[(far_up, 0, span)]],
            [[(far_down, 0, span)]],
        ]
    )
    up2, down2 = moved(up, dy=1), moved(down, dy=-1)
    rest_z = moved(rest, dz=HALF_Z)
    zfb, zfa = moved(far_up, dz=2), moved(far_down, dz=-2)

    up, down, rest_pair = assemble(
        [
            [[(up2, span, span)], [(up2, span + full, span)], [(zfb, 0, span)], [(zfa, 0, span)]],
            [
                [(down2, 2 * span, span)],
                [(down2, 2 * span + full, span)],
                [(zfb, 0, span)],
                [(zfa, 0, span)],
            ],
            [[(own[1], 0, u)], [(rest_z, 0, u)], [(own[2], 0, u)], [(rest_z, u, u)]],
        ]
    )
    up3, down3 = moved(up, dy=1), moved(down, dy=-1)
    rest_weights = over_x(rest_pair)
    up, down = assemble([[[(up3, 2 * span, span)]], [[(down3, 3 * span, span)]]])
    up4, down4 = moved(up, dy=1), moved(down, dy=-1)
    def cuts(*places, rows=span):
        return [[(array, start, rows)] for array, start in places]

    x_recipe = cuts((near, 0), (near_below, 0), (near_above, 0), (up2, 0))
    d_recipe = cuts((near, span), (near_below, span), (near_above, span), (down2, 0))
    for i, held in enumerate((zb, za)):
        at = span + i * full
        x_recipe += cuts((held, 0), (up2, at), (down2, at), (up3, i * span))
        d_recipe += cuts((held, span), (up2, at + span), (down2, at + span), (down3, i * span))
    lasts = [(zfb, 0), (zfa, 0)]
    lasts += [(v, at) for v in (up3, down3) for at in (full, full + span)]
    lasts += [(up4, 0), (down4, 0)]
    for (one, at), (two, to) in zip(lasts[::2], lasts[1::2]):
        x_recipe.append([(one, at, CAP), (two, to, CAP)])
        d_recipe.append([(one, at + CAP, CAP), (two, to + CAP, CAP)])
    own_x = lax.axis_index("dp") // 2
    x_rows, d_rows, grad_gate, grad_up, activated = forward(
        x_recipe, d_recipe, gate_weights, rest_weights, own_x
    )
    parts = [
        weight_grads(grad_gate, x_rows),
        weight_grads(grad_up, x_rows),
        weight_grads(activated, d_rows),
    ]

    optimizer = (master_rows, moment_one[0], moment_two[0])
    arrived = [ring_scatter(part) for part in parts]
    dec_packed = held_back(dec_packed, [up4, down4])
    dec_rows = lax.all_to_all(
        dec_packed.reshape(groups, 2 * depth, width // 2), "group", 0, 0, tiled=True
    )
    terms = [(*arrived[i], parts[i]) for i in range(3)]
    *done, fresh = adam(0, terms[:1], *optimizer, [], [])
    rollout = [jnp.concatenate(ring_gather(fresh, "dy"), 0)]
    dec_rows = held_back(dec_rows, [fresh])
    *done, fresh = adam(1, terms[1:], *optimizer, done, [])
    held, below, above, far_first, far_second = ring_gather(fresh, "dy")
    rollout.append(jnp.concatenate([held[:u], below[:u], above[:u], far_first], 0))
    rollout.append(jnp.concatenate([held[u:], below[u:], above[u:], far_second], 0))

    dec_rows = dec_rows.reshape(2 * dec_slots, width // 2)

    def both_halves(units):
        first, second = (
            contract_rows(dec_rows, units[:, at * (width // 2) : (at + 1) * (width // 2)]).reshape(
                groups, 2, depth, -1
            )[:, at]
            for at in range(2)
        )
        return (first + second).reshape(dec_slots, -1)

    dec_gate, dec_up = both_halves(rollout[0]), both_halves(rollout[1])
    dec_act = (silu_parts(dec_gate)[0] * dec_up).astype(jnp.bfloat16)
    partial = jnp.dot(dec_act, rollout[2], preferred_element_type=jnp.float32).astype(jnp.bfloat16)
    out_width = width // replicas
    padded = -(-out_width // 128) * 128
    partial = partial.reshape(groups, depth, replicas, out_width).transpose(0, 2, 1, 3)
    partial = jnp.pad(partial, ((0, 0), (0, 0), (0, 0), (0, padded - out_width)))
    partial = partial.reshape(groups * replicas, depth * padded // 128, 128)
    returned = lax.all_to_all(partial, ALL, 0, 0, tiled=True)
    returned = returned.reshape(groups, replicas, depth, padded).astype(jnp.float32)
    expert_out = jnp.sum(returned, 1)[..., :out_width].astype(jnp.bfloat16)
    expert_out = expert_out.reshape(dec_slots, out_width)
    picked = lax.dot_general(
        dec_select, expert_out, (((0,), (0,)), ((), ())), preferred_element_type=jnp.float32
    ).reshape(steps, dec_dev, out_width)
    dec_out = (dec_scale * picked).astype(jnp.bfloat16)
    return (*(value[None] for value in done), dec_out)


def solution(mesh):
    in_specs = (
        P(("group", "dp"), None),
        P(("group", "dp"), None),
        P(("group", "dp"), None),
        P(("group", "dp"), None),
        P("group", "dp", None),
        P("group", "dp", None),
        P("group", "dp", None),
        P(None, "group", None),
        P(None, "group", None),
        P(None, "group", None),
    )
    out_specs = (
        P("group", "dp", None),
        P("group", "dp", None),
        P("group", "dp", None),
        P(None, "group", "dp"),
    )
    return jax.shard_map(shards, mesh=mesh, in_specs=in_specs, out_specs=out_specs, check_vma=False)
```

```python
import functools

import jax
import jax.numpy as jnp
from jax import lax
from jax.experimental import pallas as pl
from jax.experimental.pallas import tpu as pltpu
from jax.sharding import PartitionSpec as P

EXPERTS = 8
CAP = 24
DCAP = 4
NY, NZ, NC, NX = 4, 8, 2, 4
HALF_Z = 4
ALL = ("group", "dp")

adam_lr = 0.001
beta_one = 0.9
beta_two = 0.95
adam_eps = 1e-08
decay_rate = 0.1
step_count = 100.0


def device_at(y, z, c, x):
    y, z, x = y % NY, z % NZ, x % NX
    group = (y * HALF_Z + z % HALF_Z) * NC + c
    return group * (NX * 2) + x * 2 + z // HALF_Z


def moved(value, dy=0, dz=0, swap_core=False, dx=0):
    pairs = []
    for y in range(NY):
        for z in range(NZ):
            for c in range(NC):
                for x in range(NX):
                    target = device_at(y + dy, z + dz, 1 - c if swap_core else c, x + dx)
                    pairs.append((device_at(y, z, c, x), target))
    return lax.ppermute(value, ALL, pairs)


def silu_parts(values):
    sig = jax.nn.sigmoid(values)
    return (values * sig, sig * (1.0 + values * (1.0 - sig)))


def rank_within(route_ids, experts, axis_dim):
    onehot = (route_ids[..., None] == jnp.arange(experts, dtype=jnp.int32)).astype(jnp.int32)
    running = jnp.cumsum(onehot, axis=axis_dim) - 1
    return jnp.sum(running * onehot, axis=-1)


def contract_rows(left, right):
    return lax.dot_general(
        left, right, (((1,), (1,)), ((), ())), preferred_element_type=jnp.float32
    )


def assemble(recipes, after=()):
    arrays, places = [], {}
    for recipe in recipes:
        for segment in recipe:
            for array, _, _ in segment:
                if id(array) not in places:
                    places[id(array)] = len(arrays)
                    arrays.append(array)
    heights = [sum(segment[0][2] for segment in recipe) for recipe in recipes]
    count = len(arrays) + len(after)
    width = arrays[0].shape[1]
    blocks = 2

    def columns(rows):
        return pl.BlockSpec((rows, width // blocks), lambda i: (0, i))

    def body(*refs):
        for out, recipe in enumerate(recipes):
            at = 0
            for segment in recipe:
                values = [refs[places[id(v)]][start : start + rows] for v, start, rows in segment]
                if len(values) > 1:
                    total = values[0].astype(jnp.float32)
                    for value in values[1:]:
                        total += value.astype(jnp.float32)
                    values = [total.astype(jnp.bfloat16)]
                rows = segment[0][2]
                refs[count + out][at : at + rows] = values[0]
                at += rows

    return pl.pallas_call(
        body,
        grid=(blocks,),
        in_specs=[columns(v.shape[0]) for v in arrays]
        + [pl.BlockSpec(memory_space=pl.ANY)] * len(after),
        out_specs=[columns(h) for h in heights],
        out_shape=[jax.ShapeDtypeStruct((h, width), jnp.bfloat16) for h in heights],
        compiler_params=pltpu.CompilerParams(vmem_limit_bytes=60 * 1024 * 1024),
        cost_estimate=pl.CostEstimate(
            flops=0, bytes_accessed=4 * sum(heights) * width, transcendentals=0
        ),
        name="assemble",
    )(*arrays, *after)


def held_back(value, after):
    def body(*refs):
        del refs

    anywhere = pl.BlockSpec(memory_space=pl.ANY)
    return pl.pallas_call(
        body,
        in_specs=[anywhere] * (1 + len(after)),
        out_specs=anywhere,
        out_shape=jax.ShapeDtypeStruct(value.shape, value.dtype),
        input_output_aliases={0: 0},
        cost_estimate=pl.CostEstimate(flops=0, bytes_accessed=0, transcendentals=0),
        name="held_back",
    )(value, *after)


def pack_block(cap, select_ref, x_own, x_other, d_own, d_other, near, up, down, far_up, far_down):
    pairs = []
    for own, other in ((x_own, x_other), (d_own, d_other)):
        rows = jnp.concatenate([own[...], other[...]], 0)
        pairs.append(jnp.dot(select_ref[...], rows, preferred_element_type=jnp.float32))
    span = 2 * cap
    for out, at in ((near, 0), (up, 1), (down, 3)):
        out[:span] = pairs[0][at * span : (at + 1) * span].astype(jnp.bfloat16)
        out[span:] = pairs[1][at * span : (at + 1) * span].astype(jnp.bfloat16)
    for out, at in ((far_up, 2 * span), (far_down, 2 * span + cap)):
        out[...] = jnp.concatenate([v[at : at + cap] for v in pairs], 0).astype(jnp.bfloat16)


def pack(cap, select, *rows):
    width = rows[0].shape[1]
    blocks = 2
    block = width // blocks

    def columns(count):
        return pl.BlockSpec((count, block), lambda i: (0, i))

    heights = [4 * cap, 4 * cap, 4 * cap, 2 * cap, 2 * cap]
    return pl.pallas_call(
        functools.partial(pack_block, cap),
        grid=(blocks,),
        in_specs=[pl.BlockSpec(select.shape, lambda i: (0, 0))] + [columns(v.shape[0]) for v in rows],
        out_specs=[columns(h) for h in heights],
        out_shape=[jax.ShapeDtypeStruct((h, width), jnp.bfloat16) for h in heights],
        cost_estimate=pl.CostEstimate(
            flops=4 * select.size * width, bytes_accessed=2 * (4 * 128 + sum(heights)) * width, transcendentals=0
        ),
        name="pack",
    )(select, *rows)


def forward_block(places, count, own_x_ref, *refs):
    pieces, gate_ref, rest_ref = refs[:count], refs[count], refs[count + 1]
    outs, sums = refs[count + 2 : -3], refs[-3:]
    step = pl.program_id(0)
    for out, recipe in zip(outs[:2], places):
        at = 0
        for segment in recipe:
            values = [pieces[i][start : start + rows] for i, start, rows in segment]
            if len(values) > 1:
                values = [v.astype(jnp.float32) for v in values]
                values = [jnp.concatenate(values, 0).astype(jnp.bfloat16)]
            out[at : at + values[0].shape[0]] = values[0]
            at += values[0].shape[0]
    unit = rest_ref.shape[0] // (2 * NX)
    parts = [gate_ref[...]]
    for i in range(2):
        cuts = [rest_ref[(2 * x + i) * unit : (2 * x + i + 1) * unit] for x in range(NX)]
        parts.append(jnp.concatenate(cuts, 0))
    for total, part, rows in zip(sums, parts, (outs[0], outs[0], outs[1])):
        product = contract_rows(part, rows[...])

        @pl.when(step == 0)
        def _():
            total[...] = product

        @pl.when(step > 0)
        def _():
            total[...] += product

    @pl.when(step == pl.num_programs(0) - 1)
    def _():
        for x in range(NX):
            cut = slice(x * unit, (x + 1) * unit)
            gate_pre, up_pre, back_pre = (total[cut] for total in sums)
            silu_val, silu_grad = silu_parts(gate_pre)
            ahead = (x - own_x_ref[0] + NX) % NX
            to = pl.ds(pl.multiple_of(ahead * unit, unit), unit)
            outs[2][to] = (back_pre * up_pre * silu_grad).astype(jnp.bfloat16)
            outs[3][to] = (back_pre * silu_val).astype(jnp.bfloat16)
            outs[4][to] = (silu_val * up_pre).astype(jnp.bfloat16)


def forward(x_recipe, d_recipe, gate, rest, own_x):
    arrays, index = [], {}
    for recipe in (x_recipe, d_recipe):
        for segment in recipe:
            for array, _, _ in segment:
                if id(array) not in index:
                    index[id(array)] = len(arrays)
                    arrays.append(array)
    places = [
        [[(index[id(v)], start, rows) for v, start, rows in segment] for segment in recipe]
        for recipe in (x_recipe, d_recipe)
    ]
    height = sum(rows for segment in x_recipe for _, _, rows in segment)
    units, width = gate.shape
    blocks = 2

    def columns(rows):
        return pl.BlockSpec((rows, width // blocks), lambda i: (0, i))

    whole = pl.BlockSpec((units, height), lambda i: (0, 0))
    rows_shape = jax.ShapeDtypeStruct((height, width), jnp.bfloat16)
    return pl.pallas_call(
        functools.partial(forward_block, places, len(arrays)),
        grid=(blocks,),
        in_specs=[pl.BlockSpec(memory_space=pltpu.SMEM)]
        + [columns(v.shape[0]) for v in (*arrays, gate, rest)],
        out_specs=[columns(height)] * 2 + [whole] * 3,
        out_shape=[rows_shape] * 2 + [jax.ShapeDtypeStruct((units, height), jnp.bfloat16)] * 3,
        scratch_shapes=[pltpu.VMEM((units, height), jnp.float32)] * 3,
        compiler_params=pltpu.CompilerParams(vmem_limit_bytes=60 * 1024 * 1024),
        cost_estimate=pl.CostEstimate(
            flops=6 * units * height * width, bytes_accessed=10 * height * width, transcendentals=0
        ),
        name="forward",
    )(own_x.reshape(1), *arrays, gate, rest)


def weight_block(source_ref, rows_ref, out_ref):
    out_ref[...] = jnp.dot(
        source_ref[...], rows_ref[...], preferred_element_type=jnp.float32
    ).astype(jnp.bfloat16)


def weight_grads(source, rows):
    units, height = source.shape
    width = rows.shape[1]
    blocks = 1
    return pl.pallas_call(
        weight_block,
        grid=(blocks,),
        in_specs=[
            pl.BlockSpec((units, height), lambda i: (0, 0)),
            pl.BlockSpec((height, width // blocks), lambda i: (0, i)),
        ],
        out_specs=pl.BlockSpec((units, width // blocks), lambda i: (0, i)),
        out_shape=jax.ShapeDtypeStruct((units, width), jnp.bfloat16),
        compiler_params=pltpu.CompilerParams(vmem_limit_bytes=32 * 1024 * 1024),
        cost_estimate=pl.CostEstimate(
            flops=2 * units * height * width,
            bytes_accessed=2 * (units + height) * width,
            transcendentals=0,
        ),
        name="weight_grads",
    )(source, rows)


def ring_gather(value, axis):
    half = value.shape[0] // 2
    below = moved(value, **{axis: 1})
    above = moved(value, **{axis: -1})
    far_first = moved(below[:half], **{axis: 1})
    far_second = moved(above[half:], **{axis: -1})
    return [value, below, above, far_first, far_second]


def ring_scatter(part):
    rows = part.shape[0] // 4
    half = rows // 2

    def added(*terms):
        return sum(v.astype(jnp.float32) for v in terms).astype(jnp.bfloat16)

    via_above = moved(part[2 * rows : 2 * rows + half], dx=1)
    via_below = moved(part[2 * rows + half : 3 * rows], dx=-1)
    up_first = added(part[rows : rows + half], via_above)
    down_second = added(part[3 * rows + half :], via_below)
    below = moved(jnp.concatenate([up_first, part[rows + half : 2 * rows]], 0), dx=1)
    above = moved(jnp.concatenate([part[3 * rows : 3 * rows + half], down_second], 0), dx=-1)
    other = moved(added(part[half:rows], below[half:], above[half:]), dz=HALF_Z)
    return below, above, other


def adam_block(count, *refs):
    held_ref, one_ref, two_ref = refs[4 * count : 4 * count + 3]
    new_held_ref, new_one_ref, new_two_ref, rollout_ref = refs[-4:]
    rows = rollout_ref.shape[0]

    def update(terms):
        grads = sum(ref[:rows].astype(jnp.float32) for ref in terms)
        one = beta_one * one_ref[...] + (1.0 - beta_one) * grads
        two = beta_two * two_ref[...] + (1.0 - beta_two) * grads * grads
        correct_one = 1.0 - beta_one**step_count
        correct_two = 1.0 - beta_two**step_count
        change = one / correct_one / (jnp.sqrt(two / correct_two) + adam_eps)
        held = held_ref[...]
        held = held - adam_lr * (change + decay_rate * held)
        new_held_ref[...] = held
        new_one_ref[...] = one
        new_two_ref[...] = two
        rollout_ref[...] = held.astype(jnp.bfloat16)

    for i in range(count):
        terms = refs[4 * i : 4 * i + 4]
        if count == 1:
            update(terms)
        else:
            pl.when(pl.program_id(0) == i)(functools.partial(update, terms))


def adam(first, terms, held, one, two, done, after):
    rows, width = held.shape[0], terms[0][0].shape[1]
    flat = [v for four in terms for v in four]
    ours = pl.BlockSpec((rows, width), lambda i: (0, first + i))
    full = jax.ShapeDtypeStruct(held.shape, jnp.float32)
    kept = len(flat) + 3
    return pl.pallas_call(
        functools.partial(adam_block, len(terms)),
        grid=(len(terms),),
        in_specs=[pl.BlockSpec((rows, width), lambda i: (0, 0))] * len(flat)
        + [ours] * 3
        + [pl.BlockSpec(memory_space=pl.ANY)] * (len(done) + len(after)),
        out_specs=[ours] * 3 + [pl.BlockSpec((rows, width), lambda i: (i, 0))],
        out_shape=[full] * 3 + [jax.ShapeDtypeStruct((len(terms) * rows, width), jnp.bfloat16)],
        input_output_aliases={kept + i: i for i in range(len(done))},
        compiler_params=pltpu.CompilerParams(vmem_limit_bytes=32 * 1024 * 1024),
        cost_estimate=pl.CostEstimate(
            flops=20 * len(terms) * rows * width,
            bytes_accessed=32 * len(terms) * rows * width,
            transcendentals=0,
        ),
        name="adam",
    )(*flat, held, one, two, *done, *after)


def shards(
    tokens,
    routes,
    gate_scale,
    cotangent,
    master,
    moment_one,
    moment_two,
    dec_tokens,
    dec_routes,
    dec_scale,
):
    replicas = lax.axis_size("dp")
    groups = lax.axis_size("group")
    width = tokens.shape[1]
    own_group = lax.axis_index("group")
    own_expert = own_group % EXPERTS
    own_z, own_c = own_expert // NC, own_expert % NC

    per_peer = DCAP // NY
    steps, dec_dev = dec_tokens.shape[0], dec_tokens.shape[1]
    dec_ids = dec_routes[..., 0]
    dec_slot = rank_within(dec_ids, EXPERTS, 1)
    block = (dec_slot // per_peer + own_group) % NY
    target = block * EXPERTS + dec_ids
    depth = steps * per_peer
    dec_slots = groups * depth
    dec_step = jnp.arange(steps, dtype=jnp.int32)[:, None]
    dec_place = dec_step * per_peer + dec_slot % per_peer
    dec_position = (target * depth + dec_place).reshape(steps * dec_dev)
    dec_select = (
        jnp.arange(dec_slots, dtype=jnp.int32)[:, None] == dec_position[None, :]
    ).astype(jnp.bfloat16)
    half_position = (target * 2 * depth + dec_place).reshape(steps * dec_dev)
    half_select = (
        jnp.arange(2 * dec_slots, dtype=jnp.int32)[:, None]
        == jnp.concatenate([half_position, half_position + depth])[None, :]
    ).astype(jnp.bfloat16)
    dec_flat = dec_tokens.reshape(steps * dec_dev, width)
    dec_packed = jnp.dot(
        half_select,
        jnp.concatenate([dec_flat[:, : width // 2], dec_flat[:, width // 2 :]], 0),
        preferred_element_type=jnp.float32,
    ).astype(jnp.bfloat16)

    scaled = (gate_scale * cotangent.astype(jnp.float32)).astype(jnp.bfloat16)
    route_ids = routes[:, 0]
    slot = rank_within(route_ids, EXPERTS, 0)
    ahead = (route_ids // NC - own_z) % HALF_Z
    position = ahead * (2 * CAP) + slot
    same_core = route_ids % NC == own_c
    position_own = jnp.where(same_core, position, -1)
    position_other = moved(jnp.where(same_core, -1, position + CAP)[None], swap_core=True)[0]
    tokens_other = moved(tokens, swap_core=True)
    scaled_other = moved(scaled, swap_core=True)
    positions = jnp.concatenate([position_own, position_other])
    select = (
        jnp.arange(HALF_Z * 2 * CAP, dtype=jnp.int32)[:, None] == positions[None, :]
    ).astype(jnp.bfloat16)
    near, step_up, step_down, far_up, far_down = pack(
        CAP, select, tokens, tokens_other, scaled, scaled_other
    )
    span = 2 * CAP
    full = 2 * span

    master_rows = master[0]
    own = [
        master_rows[:, part * width : (part + 1) * width].astype(jnp.bfloat16) for part in range(3)
    ]
    u = own[0].shape[0]
    gate_z = moved(own[0], dz=HALF_Z)

    along_x = [[x * 2 + half for x in range(NX)] for half in range(2)]

    def over_x(value):
        return lax.all_gather(value, "dp", axis=0, tiled=True, axis_index_groups=along_x)

    near_below, near_above = moved(near, dy=1), moved(near, dy=-1)
    zb, za = moved(step_up, dz=1), moved(step_down, dz=-1)
    (gate_pair,) = assemble([[[(own[0], 0, u)], [(gate_z, 0, u)]]], [near])
    gate_weights = over_x(gate_pair)

    up, down, rest, far_up, far_down = assemble(
        [
            [[(near_below, 0, span)], [(zb, 0, full)], [(za, 0, full)]],
            [[(near_above, span, span)], [(zb, 0, full)], [(za, 0, full)]],
            [[(own[1], 0, u)], [(own[2], 0, u)]],
            [[(far_up, 0, span)]],
            [[(far_down, 0, span)]],
        ]
    )
    up2, down2 = moved(up, dy=1), moved(down, dy=-1)
    rest_z = moved(rest, dz=HALF_Z)
    zfb, zfa = moved(far_up, dz=2), moved(far_down, dz=-2)

    up, down, rest_pair = assemble(
        [
            [[(up2, span, span)], [(up2, span + full, span)], [(zfb, 0, span)], [(zfa, 0, span)]],
            [
                [(down2, 2 * span, span)],
                [(down2, 2 * span + full, span)],
                [(zfb, 0, span)],
                [(zfa, 0, span)],
            ],
            [[(own[1], 0, u)], [(rest_z, 0, u)], [(own[2], 0, u)], [(rest_z, u, u)]],
        ]
    )
    up3, down3 = moved(up, dy=1), moved(down, dy=-1)
    rest_weights = over_x(rest_pair)
    up, down = assemble([[[(up3, 2 * span, span)]], [[(down3, 3 * span, span)]]])
    up4, down4 = moved(up, dy=1), moved(down, dy=-1)
    def cuts(*places, rows=span):
        return [[(array, start, rows)] for array, start in places]

    x_recipe = cuts((near, 0), (near_below, 0), (near_above, 0), (up2, 0))
    d_recipe = cuts((near, span), (near_below, span), (near_above, span), (down2, 0))
    for i, held in enumerate((zb, za)):
        at = span + i * full
        x_recipe += cuts((held, 0), (up2, at), (down2, at), (up3, i * span))
        d_recipe += cuts((held, span), (up2, at + span), (down2, at + span), (down3, i * span))
    lasts = [(zfb, 0), (zfa, 0)]
    lasts += [(v, at) for v in (up3, down3) for at in (full, full + span)]
    lasts += [(up4, 0), (down4, 0)]
    for (one, at), (two, to) in zip(lasts[::2], lasts[1::2]):
        x_recipe.append([(one, at, CAP), (two, to, CAP)])
        d_recipe.append([(one, at + CAP, CAP), (two, to + CAP, CAP)])
    own_x = lax.axis_index("dp") // 2
    x_rows, d_rows, grad_gate, grad_up, activated = forward(
        x_recipe, d_recipe, gate_weights, rest_weights, own_x
    )
    parts = [
        weight_grads(grad_gate, x_rows),
        weight_grads(grad_up, x_rows),
        weight_grads(activated, d_rows),
    ]

    optimizer = (master_rows, moment_one[0], moment_two[0])
    arrived = [ring_scatter(part) for part in parts]
    dec_packed = held_back(dec_packed, [up4, down4])
    dec_rows = lax.all_to_all(
        dec_packed.reshape(groups, 2 * depth, width // 2), "group", 0, 0, tiled=True
    )
    terms = [(*arrived[i], parts[i]) for i in range(3)]
    *done, fresh = adam(0, terms[:1], *optimizer, [], [])
    rollout = [jnp.concatenate(ring_gather(fresh, "dy"), 0)]
    dec_rows = held_back(dec_rows, [fresh])
    *done, fresh = adam(1, terms[1:], *optimizer, done, [])
    held, below, above, far_first, far_second = ring_gather(fresh, "dy")
    rollout.append(jnp.concatenate([held[:u], below[:u], above[:u], far_first], 0))
    rollout.append(jnp.concatenate([held[u:], below[u:], above[u:], far_second], 0))

    dec_rows = dec_rows.reshape(2 * dec_slots, width // 2)

    def both_halves(units):
        first, second = (
            contract_rows(dec_rows, units[:, at * (width // 2) : (at + 1) * (width // 2)]).reshape(
                groups, 2, depth, -1
            )[:, at]
            for at in range(2)
        )
        return (first + second).reshape(dec_slots, -1)

    dec_gate, dec_up = both_halves(rollout[0]), both_halves(rollout[1])
    dec_act = (silu_parts(dec_gate)[0] * dec_up).astype(jnp.bfloat16)
    partial = jnp.dot(dec_act, rollout[2], preferred_element_type=jnp.float32).astype(jnp.bfloat16)
    out_width = width // replicas
    padded = -(-out_width // 128) * 128
    partial = partial.reshape(groups, depth, replicas, out_width).transpose(0, 2, 1, 3)
    partial = jnp.pad(partial, ((0, 0), (0, 0), (0, 0), (0, padded - out_width)))
    partial = partial.reshape(groups * replicas, depth * padded // 128, 128)
    returned = lax.all_to_all(partial, ALL, 0, 0, tiled=True)
    returned = returned.reshape(groups, replicas, depth, padded).astype(jnp.float32)
    expert_out = jnp.sum(returned, 1)[..., :out_width].astype(jnp.bfloat16)
    expert_out = expert_out.reshape(dec_slots, out_width)
    picked = lax.dot_general(
        dec_select, expert_out, (((0,), (0,)), ((), ())), preferred_element_type=jnp.float32
    ).reshape(steps, dec_dev, out_width)
    dec_out = (dec_scale * picked).astype(jnp.bfloat16)
    return (*(value[None] for value in done), dec_out)


def solution(mesh):
    in_specs = (
        P(("group", "dp"), None),
        P(("group", "dp"), None),
        P(("group", "dp"), None),
        P(("group", "dp"), None),
        P("group", "dp", None),
        P("group", "dp", None),
        P("group", "dp", None),
        P(None, "group", None),
        P(None, "group", None),
        P(None, "group", None),
    )
    out_specs = (
        P("group", "dp", None),
        P("group", "dp", None),
        P("group", "dp", None),
        P(None, "group", "dp"),
    )
    return jax.shard_map(shards, mesh=mesh, in_specs=in_specs, out_specs=out_specs, check_vma=False)
```
